256 devices in a mesh: row: 8 (over y, core), col: 32 (over z, x).
Axes of the slice: x: 4, y: 4, z: 8, core: 2. Of those that a mesh axis runs over, the one named last changes fastest.
Arguments:
- tokens: bfloat16 [768, 8192], P('col', 'row'), may hold values from -6 to 6
- grad_out: bfloat16 [768, 8192], P('col', 'row'), may hold values from -6 to 6
- w_gate: bfloat16 [8192, 16384], P('row', 'col'), may hold values from -0.125 to 0.125
- w_up: bfloat16 [8192, 16384], P('row', 'col'), may hold values from -0.125 to 0.125
- w_down: bfloat16 [16384, 8192], P('col', 'row'), may hold values from -0.09375 to 0.09375
- block_flags: int32 [64, 128], P('row', 'col'), may hold values from 0 to 1, as said below
- token_order: int32 [768], replicated, may hold values from 0 to 767, each once
Outputs:
- grad_in: bfloat16 [768, 8192], P('col', 'row')
- grad_gate: bfloat16 [8192, 16384], P('row', 'col')
- grad_up: bfloat16 [8192, 16384], P('row', 'col')
- grad_down: bfloat16 [16384, 8192], P('col', 'row')
The draws below stay inside these ranges and needn't reach their ends.
Inputs may be any that keep to these rules, and one draw needn't show every extreme that they name: `block_flags`: within the tile of blocks of one device (8192 / 8 by 16384 / 32 features) at most 16 flags are 1, and some tile has exactly 16. `token_order`: A permutation of the token rows.
All inputs are finite; a program needn't handle non-finite values.
Results may differ from the reference program's by a relative error of at most 0.034.
Values may be sent and summed in bfloat16 or wider, within the bound.
A program may use at most 128 MiB of HBM per device.

```python
import jax
import jax.numpy as jnp
from jax import lax

D = 8192
FF = 16384
BLK = 128
TOKENS = 768
NZMAX = 16
N_ROW = 8
N_COL = 32


def draw_block_flags(key, part):
    key = jax.random.fold_in(key, 11)
    heat_key, noise_key, count_key, hot_key = jax.random.split(key, 4)
    nbd = D // BLK // N_ROW
    nbf = FF // BLK // N_COL
    tile = nbd * nbf
    most = tile // 2
    heat = jax.random.randint(heat_key, (FF // BLK,), 0, 4)
    noise = jax.random.randint(noise_key, (D // BLK, FF // BLK), 0, 64)
    score = noise + 48 * heat[None, :]
    score = score.reshape(N_ROW, nbd, N_COL, nbf).transpose(0, 2, 1, 3).reshape(N_ROW, N_COL, tile)
    score = score * tile + jnp.arange(tile, dtype=jnp.int32)
    rank = jnp.argsort(jnp.argsort(-score, axis=-1, stable=True), axis=-1, stable=True)
    counts = jax.random.randint(count_key, (N_ROW, N_COL), 1, most + 1)
    hot = jax.random.randint(hot_key, (), 0, N_ROW * N_COL)
    places = jnp.arange(N_ROW * N_COL, dtype=jnp.int32).reshape(N_ROW, N_COL)
    counts = jnp.where(places == hot, most, counts)
    flags = (rank < counts[:, :, None]).astype(jnp.int32)
    return flags.reshape(N_ROW, N_COL, nbd, nbf).transpose(0, 2, 1, 3).reshape(D // BLK, FF // BLK)


def block_scale(key, shape, cuts, least, largest):
    def one(position, blocks):
        steps = jax.random.uniform(jax.random.fold_in(jax.random.fold_in(key, 6), position), (blocks,), jnp.float32, least / len(cuts), largest / len(cuts))
        return jnp.repeat(jnp.exp(steps), shape[position] // blocks).reshape((-1,) + (1,) * (len(shape) - position - 1))

    loudness = one(*cuts[0])
    for cut in cuts[1:]:
        loudness = loudness * one(*cut)
    return loudness


def scatter_about(key, dims, spread, limit, cuts=(), kind=jnp.bfloat16):
    entries = spread * jax.random.normal(key, dims, jnp.float32)
    if cuts:
        entries = entries * block_scale(key, dims, cuts, -0.22, 0.18)
    return jnp.clip(entries, -limit, limit).astype(kind)


def setup_inputs(seed: int = 0) -> dict:
    seeds = jax.random.split(jax.random.key(seed), 8)
    return {
        "tokens": scatter_about(seeds[0], (TOKENS, D), 1.0, 6.0, ((0, 32), (1, 8))),
        "grad_out": scatter_about(seeds[1], (TOKENS, D), 1.0, 6.0, ((0, 32), (1, 8))),
        "w_gate": scatter_about(seeds[2], (D, FF), (D // 4) ** -0.5, 0.125, ((0, 8), (1, 32))),
        "w_up": scatter_about(seeds[3], (D, FF), (D // 4) ** -0.5, 0.125, ((0, 8), (1, 32))),
        "w_down": scatter_about(seeds[4], (FF, D), (FF // 4) ** -0.5, 0.09375, ((0, 32), (1, 8))),
        "block_flags": draw_block_flags(jax.random.fold_in(seeds[7], 71), 0),
        "token_order": jax.random.permutation(seeds[6], TOKENS).astype(jnp.int32),
    }


def slot_tables(flag_tile, count):
    nbd, nbf = flag_tile.shape
    flat = flag_tile.reshape(-1)
    slots = jnp.argsort(-flat, stable=True)[:count].astype(jnp.int32)
    valid = flat[slots].astype(jnp.float32)
    row_block = slots // nbf
    col_block = slots % nbf
    onehot_d = (row_block[:, None] == jnp.arange(nbd, dtype=jnp.int32)[None, :]).astype(jnp.float32)
    onehot_f = (col_block[:, None] == jnp.arange(nbf, dtype=jnp.int32)[None, :]).astype(jnp.float32)
    return row_block, col_block, valid, onehot_d, onehot_f


def reference(tokens, grad_out, w_gate, w_up, w_down, block_flags, token_order):
    dy = grad_out[token_order]
    nbd = D // N_ROW // BLK
    nbf = FF // N_COL // BLK
    width_r = D // N_ROW
    width_c = FF // N_COL
    count = NZMAX
    high = lax.Precision.HIGHEST

    def tile_parts(r, c):
        flag_tile = lax.dynamic_slice(block_flags, (r * nbd, c * nbf), (nbd, nbf))
        row_block, col_block, valid, onehot_d, onehot_f = slot_tables(flag_tile, count)
        keep = valid.astype(jnp.bfloat16)[:, None, None]
        gate_tile = lax.dynamic_slice(w_gate, (r * width_r, c * width_c), (width_r, width_c))
        up_tile = lax.dynamic_slice(w_up, (r * width_r, c * width_c), (width_r, width_c))
        down_tile = lax.dynamic_slice(w_down, (c * width_c, r * width_r), (width_c, width_r))
        gate_blocks = gate_tile.reshape(nbd, BLK, nbf, BLK)[row_block, :, col_block, :] * keep
        up_blocks = up_tile.reshape(nbd, BLK, nbf, BLK)[row_block, :, col_block, :] * keep
        down_blocks = down_tile.reshape(nbf, BLK, nbd, BLK)[col_block, :, row_block, :] * keep
        x_rows = lax.dynamic_slice_in_dim(tokens, r * width_r, width_r, 1)
        dy_rows = lax.dynamic_slice_in_dim(dy, r * width_r, width_r, 1)
        x_packed = x_rows.reshape(TOKENS, nbd, BLK)[:, row_block, :]
        dy_packed = dy_rows.reshape(TOKENS, nbd, BLK)[:, row_block, :]
        return (row_block, col_block, valid, onehot_d, onehot_f, gate_blocks, up_blocks, down_blocks, x_packed, dy_packed)

    def onto_columns(slot_vals, onehot_f):
        return jnp.einsum("tnj,nf->tfj", slot_vals, onehot_f, precision=high).reshape(TOKENS, width_c)

    def column_forward(c):
        def row_term(r):
            parts = tile_parts(r, c)
            onehot_f = parts[4]
            gate_blocks, up_blocks, down_blocks = parts[5], parts[6], parts[7]
            x_packed = parts[8].astype(jnp.float32)
            dy_packed = parts[9].astype(jnp.float32)
            gate_p = onto_columns(jnp.einsum("tnk,nkj->tnj", x_packed, gate_blocks.astype(jnp.float32)), onehot_f)
            up_p = onto_columns(jnp.einsum("tnk,nkj->tnj", x_packed, up_blocks.astype(jnp.float32)), onehot_f)
            dh_p = onto_columns(jnp.einsum("tnk,njk->tnj", dy_packed, down_blocks.astype(jnp.float32)), onehot_f)
            return gate_p.astype(jnp.bfloat16), up_p.astype(jnp.bfloat16), dh_p.astype(jnp.bfloat16)

        gate_t, up_t, dh_t = lax.map(row_term, jnp.arange(N_ROW, dtype=jnp.int32))
        gate = jnp.sum(gate_t.astype(jnp.float32), axis=0)
        up = jnp.sum(up_t.astype(jnp.float32), axis=0)
        dh = jnp.sum(dh_t.astype(jnp.float32), axis=0)
        sig = jax.nn.sigmoid(gate)
        silu = gate * sig
        hidden = (silu * up).astype(jnp.bfloat16)
        d_up = (dh * silu).astype(jnp.bfloat16)
        d_gate = (dh * up * sig * (1.0 + gate * (1.0 - sig))).astype(jnp.bfloat16)
        return hidden, d_gate, d_up

    hidden_c, d_gate_c, d_up_c = lax.map(column_forward, jnp.arange(N_COL, dtype=jnp.int32))

    def row_backward(r):
        def tile_back(c):
            parts = tile_parts(r, c)
            col_block, valid, onehot_d, onehot_f = parts[1], parts[2], parts[3], parts[4]
            gate_blocks, up_blocks = parts[5].astype(jnp.float32), parts[6].astype(jnp.float32)
            x_packed = parts[8].astype(jnp.float32)
            dy_packed = parts[9].astype(jnp.float32)
            hid = lax.dynamic_index_in_dim(hidden_c, c, 0, keepdims=False)
            dgt = lax.dynamic_index_in_dim(d_gate_c, c, 0, keepdims=False)
            dup = lax.dynamic_index_in_dim(d_up_c, c, 0, keepdims=False)
            hid_p = hid.reshape(TOKENS, nbf, BLK)[:, col_block, :].astype(jnp.float32)
            dgt_p = dgt.reshape(TOKENS, nbf, BLK)[:, col_block, :].astype(jnp.float32)
            dup_p = dup.reshape(TOKENS, nbf, BLK)[:, col_block, :].astype(jnp.float32)
            slot_dx = jnp.einsum("tnj,nkj->tnk", dgt_p, gate_blocks) + jnp.einsum("tnj,nkj->tnk", dup_p, up_blocks)
            dx_term = jnp.einsum("tnk,nd->tdk", slot_dx, onehot_d, precision=high).reshape(TOKENS, width_r)
            placed_d = onehot_d * valid[:, None]
            g_blk = jnp.einsum("tnk,tnj->nkj", x_packed, dgt_p)
            u_blk = jnp.einsum("tnk,tnj->nkj", x_packed, dup_p)
            d_blk = jnp.einsum("tnj,tnk->njk", hid_p, dy_packed)
            g_tile = jnp.einsum("nkj,nd,nf->dkfj", g_blk, placed_d, onehot_f, precision=high).reshape(width_r, width_c)
            u_tile = jnp.einsum("nkj,nd,nf->dkfj", u_blk, placed_d, onehot_f, precision=high).reshape(width_r, width_c)
            d_tile = jnp.einsum("njk,nd,nf->fjdk", d_blk, placed_d, onehot_f, precision=high).reshape(width_c, width_r)
            return (dx_term.astype(jnp.bfloat16), g_tile.astype(jnp.bfloat16), u_tile.astype(jnp.bfloat16), d_tile.astype(jnp.bfloat16))

        dx_t, g_t, u_t, d_t = lax.map(tile_back, jnp.arange(N_COL, dtype=jnp.int32))
        dx_r = jnp.sum(dx_t.astype(jnp.float32), axis=0).astype(jnp.bfloat16)
        return dx_r, g_t, u_t, d_t

    dx_all, g_all, u_all, d_all = lax.map(row_backward, jnp.arange(N_ROW, dtype=jnp.int32))
    grad_in = jnp.transpose(dx_all, (1, 0, 2)).reshape(TOKENS, D)
    grad_gate = jnp.transpose(g_all, (0, 2, 1, 3)).reshape(D, FF)
    grad_up = jnp.transpose(u_all, (0, 2, 1, 3)).reshape(D, FF)
    grad_down = jnp.transpose(d_all, (1, 2, 0, 3)).reshape(FF, D)
    return grad_in, grad_gate, grad_up, grad_down
```

```python
import functools

import jax
import jax.numpy as jnp
from jax import lax
from jax.experimental import pallas as pl
from jax.experimental.pallas import tpu as pltpu
from jax.sharding import PartitionSpec as P

MESH = pl.DeviceIdType.MESH
F32 = jnp.float32
BF16 = jnp.bfloat16

NY, NK, NZ, NX = 4, 2, 8, 4
ROWS = 24
TOK = 768
HALF = TOK // 2
DW = 1024
FW = 512
BLK = 128
SLAB = (2 * ROWS, DW // 2)


def nt(a, b):
    return lax.dot_general(a, b, (((1,), (1,)), ((), ())), preferred_element_type=F32)


def nn(a, b):
    return lax.dot_general(a, b, (((1,), (0,)), ((), ())), preferred_element_type=F32)


def kernel(tok_ref, go_ref, wg_hbm, wu_hbm, wd_hbm, flags, order,
           gin_ref, ggate_ref, gup_ref, gdown_ref,
           raw_g, raw_u, raw_d, wgu, wd, gbuf, tbuf, x_all, g_all, dy, xt, perm,
           part, crecv, ssend, yrecv, sown, dgdu, hidt, hid, dxf, rsx, xrecv, zsrc, zrecv,
           wsem, bar_unused, gx_s, gx_r, gz_s, gz_r, tz_s, tz_r, tx_s, tx_r,
           c_s, c_r, y_s, y_r, a_s, a_r, b_s, b_r, rx_s, rx_r, rz_s, rz_r):
    r = lax.axis_index("row")
    c = lax.axis_index("col")
    y, k, z, x = r // 2, lax.rem(r, 2), c // 4, lax.rem(c, 4)

    def at(dy_=0, dk=0, dz=0, dx=0):
        return (lax.rem(y + dy_ + NY, NY) * 2 + lax.rem(k + dk, 2),
                lax.rem(z + dz + NZ, NZ) * 4 + lax.rem(x + dx + NX, NX))

    started = []

    def rc(src, dst, ss, rs, dev):
        return pltpu.make_async_remote_copy(src_ref=src, dst_ref=dst, send_sem=ss, recv_sem=rs,
                                            device_id=dev, device_id_type=MESH)

    def send(src, dst, ss, rs, dev):
        cp = rc(src, dst, ss, rs, dev)
        cp.start()
        started.append(cp)

    loads = [pltpu.make_async_copy(s, d, wsem.at[i])
             for i, (s, d) in enumerate(((wg_hbm, raw_g), (wu_hbm, raw_u), (wd_hbm, raw_d)))]
    for cp in loads:
        cp.start()

    peers = ([dict(dx=d) for d in range(1, NX)] + [dict(dz=d) for d in range(1, NZ)]
             + [dict(dy_=d) for d in range(1, NY)] + [dict(dk=1)])
    bar = pltpu.get_barrier_semaphore()
    for p in peers:
        pl.semaphore_signal(bar, inc=1, device_id=at(**p), device_id_type=MESH)

    def to_slab(v):
        v = v.astype(F32)
        return jnp.concatenate([v[:, :DW // 2], v[:, DW // 2:]], axis=0).astype(BF16)

    gbuf[c] = to_slab(go_ref[...])
    tbuf[c] = to_slab(tok_ref[...])
    pl.semaphore_wait(bar, len(peers))

    def zrel(d):
        return lax.rem(z + d + 2 * NZ, NZ)

    for d in (2, 1, 3):
        send(gbuf.at[c], gbuf.at[c], gx_s.at[d - 1], gx_r.at[d - 1], at(dx=d))

    H = DW // 4

    def tz(direction, s):
        src = zrel(-direction * (s - 1)) * 4 + x
        i = (0 if direction == 1 else 4) + s - 1
        ref = tbuf.at[src]
        if s == 4:
            ref = tbuf.at[src, :, pl.ds(0 if direction == 1 else H, H)]
        return rc(ref, ref, tz_s.at[i], tz_r.at[i], at(dz=direction))

    def gz(direction, s, j):
        src = zrel(-direction * (s - 1)) * 4 + 2 * j
        i = ((0 if direction == 1 else 4) + s - 1) * 2 + j
        ref = gbuf.at[pl.ds(src, 2)]
        return rc(ref, ref, gz_s.at[i], gz_r.at[i], at(dz=direction))

    def tz_wait(direction, s):
        src = zrel(-direction * s) * 4 + x
        i = (0 if direction == 1 else 4) + s - 1
        ref = tbuf.at[src]
        if s == 4:
            ref = tbuf.at[src, :, pl.ds(0 if direction == 1 else H, H)]
        rc(ref, ref, tz_s.at[i], tz_r.at[i], at(dz=direction)).wait_recv()

    def gz_wait(direction, s, j):
        src = zrel(-direction * s) * 4 + 2 * j
        i = ((0 if direction == 1 else 4) + s - 1) * 2 + j
        ref = gbuf.at[pl.ds(src, 2)]
        rc(ref, ref, gz_s.at[i], gz_r.at[i], at(dz=direction)).wait_recv()

    def go(cp):
        cp.start()
        started.append(cp)

    def tx_send(rel):
        idx = zrel(rel) * 4 + x
        for d in (2, 1, 3):
            i = (rel % NZ) * 3 + d - 1
            send(tbuf.at[idx], tbuf.at[idx], tx_s.at[i], tx_r.at[i], at(dx=d))

    go(tz(1, 1))
    go(tz(-1, 1))
    tx_send(0)

    cols = jnp.broadcast_to(order[...], (BLK, TOK)).astype(F32).T
    lane = lax.broadcasted_iota(jnp.int32, (TOK, BLK), 1).astype(F32)
    for j in range(TOK // BLK):
        perm[:, j * BLK:(j + 1) * BLK] = jnp.where(cols == lane + float(j * BLK), 1.0, 0.0).astype(BF16)

    for d in (1, 3, 2):
        idx = z * 4 + lax.rem(x - d + NX, NX)
        rc(gbuf.at[idx], gbuf.at[idx], gx_s.at[d - 1], gx_r.at[d - 1], at(dx=d)).wait_recv()
    for j in range(2):
        go(gz(1, 1, j))
        go(gz(-1, 1, j))

    for s in range(1, 5):
        for direction in (1, -1):
            tz_wait(direction, s)
            if s < 4:
                go(tz(direction, s + 1))
                tx_send(-direction * s)
        if s == 4:
            tx_send(4)
        for j in range(2):
            for direction in (1, -1):
                if s < 4 or (j == 0) == (direction == 1):
                    gz_wait(direction, s, j)
                if s < 3 or (s == 3 and (j == 0) == (direction == 1)):
                    go(gz(direction, s + 1, j))
        if s == 1:
            for cp in loads:
                cp.wait()

            @pl.loop(0, DW // BLK)
            def _(i):
                rows = pl.ds(pl.multiple_of(i * BLK, BLK), BLK)
                for j in range(FW // BLK):
                    f = flags[i, j].astype(F32)
                    cs = slice(j * BLK, (j + 1) * BLK)
                    wgu[j, rows, :BLK] = (raw_g[rows, cs].astype(F32) * f).astype(BF16)
                    wgu[j, rows, BLK:] = (raw_u[rows, cs].astype(F32) * f).astype(BF16)
                    wd[j, :, rows] = (raw_d[cs, rows].astype(F32) * f).astype(BF16)

    for rel in range(NZ):
        for d in (1, 3, 2):
            i = rel * 3 + d - 1
            idx = zrel(rel) * 4 + lax.rem(x - d + NX, NX)
            rc(tbuf.at[idx], tbuf.at[idx], tx_s.at[i], tx_r.at[i], at(dx=d)).wait_recv()

    @pl.loop(0, NZ * NX // 2)
    def _(p):
        rows = pl.ds(pl.multiple_of(p * 2 * ROWS, 2 * ROWS), 2 * ROWS)
        for buf, dst in ((tbuf, x_all), (gbuf, g_all)):
            a = buf[2 * p].astype(F32)
            b = buf[2 * p + 1].astype(F32)
            dst[rows, :DW // 2] = jnp.concatenate([a[:ROWS], b[:ROWS]], axis=0).astype(BF16)
            dst[rows, DW // 2:] = jnp.concatenate([a[ROWS:], b[ROWS:]], axis=0).astype(BF16)

    @pl.loop(0, DW // 256)
    def _(i):
        cs = pl.ds(pl.multiple_of(i * 256, 256), 256)
        dy[:, cs] = nn(perm[...], g_all[:, cs]).astype(BF16)

    def half_rows(h):
        return pl.ds(pl.multiple_of(h * HALF, HALF), HALF)

    def partial(h, yb, slot):
        rows = half_rows(h)
        part[slot, :, :256] = nn(x_all[rows, :], wgu[yb]).astype(BF16)
        part[slot, :, 256:] = nt(dy[rows, :], wd[yb]).astype(BF16)

    def c_copy(d):
        return rc(part.at[d], crecv.at[d], c_s.at[d], c_r.at[d], at(dk=1))

    def ybof(d):
        return lax.rem(y + d, NY)

    @pl.loop(0, NY)
    def _(i):
        d = lax.rem(i + 1, NY)
        partial(1 - k, ybof(d), d)
        c_copy(d).start()

    def y_copy(d):
        return rc(ssend.at[d - 1], yrecv.at[d - 1], y_s.at[d - 1], y_r.at[d - 1], at(dy_=d))

    @pl.loop(1, NY)
    def _(d):
        partial(k, ybof(d), NY)
        c_copy(d).wait_recv()
        ssend[d - 1] = (part[NY].astype(F32) + crecv[d].astype(F32)).astype(BF16)
        y_copy(d).start()

    partial(k, y, NY)

    @pl.loop(0, DW // BLK)
    def _(i):
        cs = pl.ds(pl.multiple_of(i * BLK, BLK), BLK)
        xt[cs, :] = x_all[:, cs].astype(F32).T.astype(BF16)

    c_copy(0).wait_recv()
    for d in (1, 3, 2):
        y_copy(d).wait_recv()

    @pl.loop(0, HALF // 96)
    def _(i):
        rows = pl.ds(pl.multiple_of(i * 96, 96), 96)
        t = part[NY, rows, :].astype(F32) + crecv[0, rows, :].astype(F32)
        for j in range(3):
            t = t + yrecv[j, rows, :].astype(F32)
        gate, up, dh = t[:, :BLK], t[:, BLK:2 * BLK], t[:, 2 * BLK:]
        sig = 1.0 / (1.0 + jnp.exp(-gate))
        silu = gate * sig
        hid[rows, :] = silu * up
        dgdu[k, y, rows, :BLK] = (dh * up * sig * (1.0 + gate * (1.0 - sig))).astype(BF16)
        dgdu[k, y, rows, BLK:] = (dh * silu).astype(BF16)

    hidt[k, y] = hid[...].T.astype(BF16)

    def a_copy(d, which):
        buf = (dgdu, hidt)[which]
        i = (d - 1) * 2 + which
        return rc(buf.at[k, y], buf.at[k, y], a_s.at[i], a_r.at[i], at(dy_=d))

    def a_wait(d, which):
        buf = (dgdu, hidt)[which]
        i = (d - 1) * 2 + which
        src = lax.rem(y - d + NY, NY)
        rc(buf.at[k, src], buf.at[k, src], a_s.at[i], a_r.at[i], at(dy_=d)).wait_recv()

    def b_copy(d, which):
        buf = (dgdu, hidt)[which]
        i = d * 2 + which
        src = lax.rem(y - d + NY, NY)
        return rc(buf.at[k, src], buf.at[k, src], b_s.at[i], b_r.at[i], at(dk=1))

    def b_wait(d, which):
        buf = (dgdu, hidt)[which]
        i = d * 2 + which
        src = lax.rem(y - d + NY, NY)
        rc(buf.at[1 - k, src], buf.at[1 - k, src], b_s.at[i], b_r.at[i], at(dk=1)).wait_recv()

    for which in range(2):
        for d in (2, 1, 3):
            go(a_copy(d, which))
        go(b_copy(0, which))
    for which in range(2):
        for d in (1, 3, 2):
            a_wait(d, which)
            go(b_copy(d, which))
    for which in range(2):
        for d in (0, 1, 3, 2):
            b_wait(d, which)

    for h in range(2):
        @pl.loop(0, DW // 256)
        def _(i, h=h):
            cs = pl.ds(pl.multiple_of(i * 256, 256), 256)
            acc = nt(dgdu[h, 0], wgu[0, cs, :])
            for yb in range(1, NY):
                acc = acc + nt(dgdu[h, yb], wgu[yb, cs, :])
            dxf[h * HALF:(h + 1) * HALF, cs] = acc

    def pack(xx):
        @pl.loop(0, NZ)
        def _(zz):
            v = dxf[pl.ds(pl.multiple_of((zz * 4 + xx) * ROWS, 8), ROWS), :]
            rsx[xx, zz] = jnp.concatenate([v[:, :DW // 2], v[:, DW // 2:]], axis=0).astype(BF16)

    for d in (2, 1, 3):
        xx = lax.rem(x + d, NX)
        pack(xx)
        send(rsx.at[xx], xrecv.at[d - 1], rx_s.at[d - 1], rx_r.at[d - 1], at(dx=d))
    pack(x)

    def weight_grads(first, last):
        @pl.loop(first, last)
        def _(j):
            acc = (nn(xt[:, :HALF], dgdu[0, j]) + nn(xt[:, HALF:], dgdu[1, j]))
            cs = pl.ds(pl.multiple_of(j * BLK, BLK), BLK)
            for i in range(DW // BLK):
                f = flags[i, j].astype(F32)
                blk = acc[i * BLK:(i + 1) * BLK] * f
                ggate_ref[i * BLK:(i + 1) * BLK, cs] = blk[:, :BLK].astype(BF16)
                gup_ref[i * BLK:(i + 1) * BLK, cs] = blk[:, BLK:].astype(BF16)
            acc = nn(hidt[0, j], dy[:HALF, :]) + nn(hidt[1, j], dy[HALF:, :])
            for i in range(DW // BLK):
                f = flags[i, j].astype(F32)
                gdown_ref[cs, i * BLK:(i + 1) * BLK] = (acc[:, i * BLK:(i + 1) * BLK] * f).astype(BF16)

    weight_grads(0, 2)

    for d in (1, 3, 2):
        rc(rsx.at[0], xrecv.at[d - 1], rx_s.at[d - 1], rx_r.at[d - 1], at(dx=d)).wait_recv()

    @pl.loop(0, NZ)
    def _(zz):
        t = rsx[x, zz].astype(F32)
        for j in range(3):
            t = t + xrecv[j, zz].astype(F32)
        zsrc[zz] = t.astype(BF16)

    for d in (4, 3, 5, 2, 6, 1, 7):
        send(zsrc.at[zrel(d)], zrecv.at[d - 1], rz_s.at[d - 1], rz_r.at[d - 1], at(dz=d))

    weight_grads(2, 4)

    for d in (1, 7, 2, 6, 3, 5, 4):
        rc(zsrc.at[0], zrecv.at[d - 1], rz_s.at[d - 1], rz_r.at[d - 1], at(dz=d)).wait_recv()
    t = zsrc[z].astype(F32)
    for j in range(NZ - 1):
        t = t + zrecv[j].astype(F32)
    gin_ref[...] = jnp.concatenate([t[:ROWS], t[ROWS:]], axis=1).astype(BF16)

    for cp in started:
        cp.wait_send()
    for d in range(NY):
        c_copy(d).wait_send()
    for d in range(1, NY):
        y_copy(d).wait_send()


def on_device(tokens, grad_out, w_gate, w_up, w_down, block_flags, token_order):
    vmem = pl.BlockSpec(memory_space=pltpu.VMEM)
    smem = pl.BlockSpec(memory_space=pltpu.SMEM)
    hbm = pl.BlockSpec(memory_space=pl.ANY)
    V = pltpu.VMEM
    sem = lambda n: pltpu.SemaphoreType.DMA((n,))
    n = NZ * NX
    scratch = [
        V((DW, FW), BF16), V((DW, FW), BF16), V((FW, DW), BF16),
        V((NY, DW, 2 * BLK), BF16), V((NY, BLK, DW), BF16),
        V((n,) + SLAB, BF16), V((n,) + SLAB, BF16),
        V((TOK, DW), BF16), V((TOK, DW), BF16), V((TOK, DW), BF16),
        V((DW, TOK), BF16), V((TOK, TOK), BF16),
        V((NY + 1, HALF, 3 * BLK), BF16), V((NY, HALF, 3 * BLK), BF16),
        V((NY - 1, HALF, 3 * BLK), BF16), V((NY - 1, HALF, 3 * BLK), BF16),
        V((8, 128), F32),
        V((NK, NY, HALF, 2 * BLK), BF16), V((NK, NY, BLK, HALF), BF16),
        V((HALF, BLK), F32), V((TOK, DW), F32),
        V((NX, NZ) + SLAB, BF16), V((NX - 1, NZ) + SLAB, BF16),
        V((NZ,) + SLAB, BF16), V((NZ - 1,) + SLAB, BF16),
        sem(3), sem(1), sem(3), sem(3), sem(16), sem(16), sem(8), sem(8), sem(24), sem(24),
        sem(4), sem(4), sem(3), sem(3), sem(6), sem(6), sem(8), sem(8), sem(3), sem(3), sem(7), sem(7),
    ]
    return pl.pallas_call(
        kernel,
        out_shape=(
            jax.ShapeDtypeStruct((ROWS, DW), BF16),
            jax.ShapeDtypeStruct((DW, FW), BF16),
            jax.ShapeDtypeStruct((DW, FW), BF16),
            jax.ShapeDtypeStruct((FW, DW), BF16),
        ),
        in_specs=[vmem, vmem, hbm, hbm, hbm, smem, vmem],
        out_specs=(vmem, vmem, vmem, vmem),
        scratch_shapes=scratch,
        compiler_params=pltpu.CompilerParams(
            collective_id=0, has_side_effects=True, vmem_limit_bytes=58 * 2**20),
        name="layer_backward",
    )(tokens, grad_out, w_gate, w_up, w_down, block_flags, token_order.reshape(1, TOK))


def solution(mesh):
    return jax.shard_map(
        on_device,
        mesh=mesh,
        in_specs=(
            P("col", "row"), P("col", "row"), P("row", "col"), P("row", "col"),
            P("col", "row"), P("row", "col"), P(),
        ),
        out_specs=(P("col", "row"), P("row", "col"), P("row", "col"), P("col", "row")),
        check_vma=False,
    )
```

```python
import functools

import jax
import jax.numpy as jnp
from jax import lax
from jax.experimental import pallas as pl
from jax.experimental.pallas import tpu as pltpu
from jax.sharding import PartitionSpec as P

MESH = pl.DeviceIdType.MESH
F32 = jnp.float32
BF16 = jnp.bfloat16

NY, NK, NZ, NX = 4, 2, 8, 4
ROWS = 24
TOK = 768
HALF = TOK // 2
DW = 1024
FW = 512
BLK = 128
SLAB = (2 * ROWS, DW // 2)
PLANE = NX * ROWS
RHO = ((0, -1), (1, -2), (2, -3), (3, 4))
NQ = len(RHO)
NP = 4
SW = NX // NP


def nt(a, b):
    return lax.dot_general(a, b, (((1,), (1,)), ((), ())), preferred_element_type=F32)


def nn(a, b):
    return lax.dot_general(a, b, (((1,), (0,)), ((), ())), preferred_element_type=F32)


def kernel(tok_hbm, go_hbm, wg_hbm, wu_hbm, wd_hbm, flags, order,
           gin_hbm, ggate_hbm, gup_hbm, gdown_hbm,
           tok_ref, go_ref, gin_ref, ggate_ref, gup_ref, gdown_ref,
           raw_g, raw_u, raw_d, wgu, wd, ga, gb, ta, tb, x_all, g_all, dy, xt, perm, ocol,
           part, crecv, ssend, yrecv, dhu, dhp, dhc, dhs, dhy, dht, act, hidt, dxf, rsx, xrecv, zsrc, zrecv,
           wsem, osem, gxa_s, gxa_r, gza_s, gza_r, gzb_s, gzb_r, gxb_s, gxb_r,
           txa_s, txa_r, tza_s, tza_r, tzb_s, tzb_r, txb_s, txb_r,
           c_s, c_r, y_s, y_r, h_s, h_r, a_s, a_r, b_s, b_r, rx_s, rx_r, rz_s, rz_r):
    r = lax.axis_index("row")
    c = lax.axis_index("col")
    y, k, z, x = r // 2, lax.rem(r, 2), c // 4, lax.rem(c, 4)

    def at(dy_=0, dk=0, dz=0, dx=0):
        return (lax.rem(y + dy_ + NY, NY) * 2 + lax.rem(k + dk, 2),
                lax.rem(z + dz + NZ, NZ) * 4 + lax.rem(x + dx + NX, NX))

    def zrel(d):
        return lax.rem(z + d + 2 * NZ, NZ)

    def yrel(d):
        return lax.rem(y + d + NY, NY)

    def xrel(d):
        return lax.rem(x + d + NX, NX)

    started = []

    def rc(src, dst, ss, rs, dev):
        return pltpu.make_async_remote_copy(src_ref=src, dst_ref=dst, send_sem=ss, recv_sem=rs,
                                            device_id=dev, device_id_type=MESH)

    def go(cp):
        cp.start()
        started.append(cp)


    peers = ([dict(dx=d) for d in range(1, NX)] + [dict(dz=d) for d in (1, 7, 2, 6, 3, 5, 4)]
             + [dict(dy_=d) for d in range(1, NY)] + [dict(dk=1)])
    bar = pltpu.get_barrier_semaphore()
    for p in peers:
        pl.semaphore_signal(bar, inc=1, device_id=at(**p), device_id_type=MESH)

    loads = [pltpu.make_async_copy(s, d, wsem.at[i])
             for i, (s, d) in enumerate(((go_hbm, go_ref), (tok_hbm, tok_ref),
                                         (wd_hbm, raw_d), (wg_hbm, raw_g), (wu_hbm, raw_u)))]
    for cp in loads:
        cp.start()
    stores = []

    def store(src, dst):
        cp = pltpu.make_async_copy(src, dst, osem.at[len(stores)])
        cp.start()
        stores.append(cp)

    QW = DW // 4

    def to_slabs(ref, a, b):
        v = ref[...].astype(F32)
        a[c] = jnp.concatenate([v[:, :QW], v[:, QW:2 * QW]], axis=0).astype(BF16)
        b[c] = jnp.concatenate([v[:, 2 * QW:3 * QW], v[:, 3 * QW:]], axis=0).astype(BF16)

    loads[0].wait()
    to_slabs(go_ref, ga, gb)
    loads[1].wait()
    to_slabs(tok_ref, ta, tb)
    pl.semaphore_wait(bar, len(peers))

    class Gather:
        def __init__(self, a, b, xa_s, xa_r, za_s, za_r, zb_s, zb_r, xb_s, xb_r):
            self.a, self.b = a, b
            self.xa, self.za, self.zb, self.xb = (xa_s, xa_r), (za_s, za_r), (zb_s, zb_r), (xb_s, xb_r)

        def xa_copy(self, d, src):
            ref = self.a.at[src]
            return rc(ref, ref, self.xa[0].at[d - 1], self.xa[1].at[d - 1], at(dx=d))

        def za_copy(self, direction, s, j, src_rel):
            i = ((0 if direction == 1 else 4) + s - 1) * NP + j
            ref = self.a.at[pl.ds(zrel(src_rel) * NX + j * SW, SW)]
            return rc(ref, ref, self.za[0].at[i], self.za[1].at[i], at(dz=direction))

        def zb_copy(self, direction, s, src_rel):
            i = (0 if direction == 1 else 4) + s - 1
            src = zrel(src_rel) * NX + x
            ref = self.b.at[src]
            if s == 4:
                ref = self.b.at[src, :, pl.ds(0 if direction == 1 else QW // 2, QW // 2)]
            return rc(ref, ref, self.zb[0].at[i], self.zb[1].at[i], at(dz=direction))

        def xb_copy(self, rel, d, src):
            i = (rel % NZ) * 3 + d - 1
            ref = self.b.at[src]
            return rc(ref, ref, self.xb[0].at[i], self.xb[1].at[i], at(dx=d))

        def xb_send(self, rel):
            for d in (2, 1, 3):
                go(self.xb_copy(rel, d, zrel(rel) * NX + x))

        def xb_wait(self, rel):
            for d in (1, 3, 2):
                self.xb_copy(rel, d, zrel(rel) * NX + xrel(-d)).wait_recv()

        def start(self):
            for d in (2, 1, 3):
                go(self.xa_copy(d, c))
            go(self.zb_copy(1, 1, 0))
            go(self.zb_copy(-1, 1, 0))
            self.xb_send(0)

        def step(self, t):
            if t <= 4:
                for direction in (1, -1):
                    self.zb_copy(direction, t, -direction * t).wait_recv()
                    if t < 4:
                        go(self.zb_copy(direction, t + 1, -direction * t))
                        self.xb_send(-direction * t)
                if t == 4:
                    self.xb_send(4)
            if t == 1:
                for d in (1, 3, 2):
                    self.xa_copy(d, z * NX + xrel(-d)).wait_recv()
                for j in range(NP):
                    for direction in (1, -1):
                        go(self.za_copy(direction, 1, j, 0))
                return
            s = t - 1
            for j in range(NP):
                for direction in (1, -1):
                    mine = (j < NP // 2) == (direction == 1)
                    if s < 4 or mine:
                        self.za_copy(direction, s, j, -direction * s).wait_recv()
                    if s < 3 or (s == 3 and mine):
                        go(self.za_copy(direction, s + 1, j, -direction * s))

    G = Gather(ga, gb, gxa_s, gxa_r, gza_s, gza_r, gzb_s, gzb_r, gxb_s, gxb_r)
    T = Gather(ta, tb, txa_s, txa_r, tza_s, tza_r, tzb_s, tzb_r, txb_s, txb_r)

    def masks(i0, i1):
        @pl.loop(i0, i1)
        def _(i):
            rows = pl.ds(pl.multiple_of(i * BLK, BLK), BLK)
            for j in range(FW // BLK):
                f = flags[j, i].astype(F32)
                cs = slice(j * BLK, (j + 1) * BLK)
                wgu[j, rows, :BLK] = (raw_g[rows, cs].astype(F32) * f).astype(BF16)
                wgu[j, rows, BLK:] = (raw_u[rows, cs].astype(F32) * f).astype(BF16)
                wd[cs, rows] = (raw_d[cs, rows].astype(F32) * f).astype(BF16)

    def unslab(a, b, c0, dst, row0):
        rows = pl.ds(row0, 2 * ROWS)
        for n, buf in enumerate((a, b)):
            v, w = buf[c0].astype(F32), buf[c0 + 1].astype(F32)
            dst[rows, 2 * n * QW:(2 * n + 1) * QW] = jnp.concatenate([v[:ROWS], w[:ROWS]], axis=0).astype(BF16)
            dst[rows, (2 * n + 1) * QW:(2 * n + 2) * QW] = jnp.concatenate([v[ROWS:], w[ROWS:]], axis=0).astype(BF16)

    def rows_of(q, p):
        return slice(p * HALF + q * PLANE, p * HALF + (q + 1) * PLANE)

    def krows(q):
        return pl.ds(pl.multiple_of(k * HALF + q * PLANE, 32), PLANE)

    kplane = pl.ds(pl.multiple_of(k * PLANE, 32), PLANE)
    khalf = pl.ds(pl.multiple_of(k * HALF, HALF), HALF)

    def c_copy(q):
        sib = pl.ds(pl.multiple_of((1 - k) * PLANE, 32), PLANE)
        return rc(part.at[q, :, sib], crecv.at[q], c_s.at[q], c_r.at[q], at(dk=1))

    def stage_p(q):
        for p in range(2):
            plane = zrel(RHO[q][p])
            T.xb_wait(RHO[q][p])
            for xx in (0, 2):
                unslab(ta, tb, plane * NX + xx, x_all, p * HALF + q * PLANE + xx * ROWS)
        lhs = jnp.concatenate([x_all[rows_of(q, 0), :], x_all[rows_of(q, 1), :]], axis=0)

        @pl.loop(0, NY)
        def _(d):
            part[q, d] = nn(lhs, wgu[yrel(d)]).astype(BF16)

        go(c_copy(q))

    def y_copy(q, d):
        i = q * 3 + d - 1
        return rc(ssend.at[q, d - 1], yrecv.at[q, d - 1], y_s.at[i], y_r.at[i], at(dy_=d))

    def stage_c(q):
        c_copy(q).wait_recv()
        for d in (2, 1, 3):
            ssend[q, d - 1] = (part[q, d, kplane, :].astype(F32) + crecv[q, d].astype(F32)).astype(BF16)
            go(y_copy(q, d))

    def a_copy(q, d, src):
        i = q * 3 + d - 1
        ref = act.at[src, krows(q)]
        return rc(ref, ref, a_s.at[i], a_r.at[i], at(dy_=d))

    def b_copy(q, d, src, half):
        i = q * 4 + d
        ref = act.at[src, pl.ds(pl.multiple_of(half * HALF + q * PLANE, 32), PLANE)]
        return rc(ref, ref, b_s.at[i], b_r.at[i], at(dk=1))

    def stage_y(q):
        for d in (1, 3, 2):
            y_copy(q, d).wait_recv()
        t = part[q, 0, kplane, :].astype(F32) + crecv[q, 0].astype(F32)
        for j in range(3):
            t = t + yrecv[q, j].astype(F32)
        gate, up = t[:, :BLK], t[:, BLK:]
        dh = dht[q * PLANE:(q + 1) * PLANE, :]
        sig = 1.0 / (1.0 + jnp.exp(-gate))
        silu = gate * sig
        rows = krows(q)
        act[y, rows, :BLK] = (dh * up * sig * (1.0 + gate * (1.0 - sig))).astype(BF16)
        act[y, rows, BLK:2 * BLK] = (dh * silu).astype(BF16)
        act[y, rows, 2 * BLK:] = (silu * up).astype(BF16)
        for d in (2, 1, 3):
            go(a_copy(q, d, y))
        go(b_copy(q, 0, y, k))

    def stage_a(q):
        for d in (1, 3, 2):
            a_copy(q, d, yrel(-d)).wait_recv()
            go(b_copy(q, d, yrel(-d), k))

    def rx_copy(q, d):
        i = q * 3 + d - 1
        return rc(rsx.at[q, xrel(d)], xrecv.at[q, d - 1], rx_s.at[i], rx_r.at[i], at(dx=d))

    def stage_b(q):
        for d in (0, 1, 3, 2):
            b_copy(q, d, yrel(-d), 1 - k).wait_recv()

        @pl.loop(0, DW // 256)
        def _(i):
            cs = pl.ds(pl.multiple_of(i * 256, 256), 256)
            acc = None
            for yb in range(NY):
                lhs = jnp.concatenate([act[yb, rows_of(q, 0), :2 * BLK], act[yb, rows_of(q, 1), :2 * BLK]], axis=0)
                t = nt(lhs, wgu[yb, cs, :])
                acc = t if acc is None else acc + t
            dxf[q % 2, :, cs] = acc

        for p in range(2):
            for xx in range(NX):
                v = dxf[q % 2, p * PLANE + xx * ROWS:p * PLANE + (xx + 1) * ROWS, :]
                rsx[q, xx, p] = jnp.concatenate([v[:, :DW // 2], v[:, DW // 2:]], axis=0).astype(BF16)
        for d in (2, 1, 3):
            go(rx_copy(q, d))

    def rz_copy(rho, src):
        i = rho % NZ - 1
        return rc(src, zrecv.at[i], rz_s.at[i], rz_r.at[i], at(dz=rho))

    def stage_x(q):
        for d in (1, 3, 2):
            rx_copy(q, d).wait_recv()
        for p in range(2):
            t = rsx[q, x, p].astype(F32)
            for j in range(3):
                t = t + xrecv[q, j, p].astype(F32)
            zsrc[q, p] = t.astype(BF16)
            if RHO[q][p] != 0:
                go(rz_copy(RHO[q][p], zsrc.at[q, p]))

    def h_copy(d):
        if d == 0:
            sib = pl.ds(pl.multiple_of((1 - k) * HALF, HALF), HALF)
            return rc(dhp.at[:, sib], dhc, h_s.at[0], h_r.at[0], at(dk=1))
        return rc(dhs.at[d - 1], dhy.at[d - 1], h_s.at[d], h_r.at[d], at(dy_=d))

    def gpair(q):
        parts = []
        for p in range(2):
            plane = zrel(RHO[q][p])
            G.xb_wait(RHO[q][p])
            for xx in (0, 2):
                unslab(ga, gb, plane * NX + xx, g_all, pl.multiple_of(plane * PLANE + xx * ROWS, 2 * ROWS))
            parts.append(pl.ds(pl.multiple_of(plane * PLANE, 32), PLANE))
        lhs = jnp.concatenate([g_all[parts[0], :], g_all[parts[1], :]], axis=0)
        for i in range(2):
            t = nt(lhs, wd[i * 256:(i + 1) * 256, :]).astype(BF16)
            dhu[parts[0], i * 256:(i + 1) * 256] = t[:PLANE]
            dhu[parts[1], i * 256:(i + 1) * 256] = t[PLANE:]

    def permute():
        @pl.loop(0, DW // 256)
        def _(i):
            cs = pl.ds(pl.multiple_of(i * 256, 256), 256)
            dy[:, cs] = nn(perm[...], g_all[:, cs]).astype(BF16)

    def dh_partial():
        for i in range(2):
            t = nn(perm[...], dhu[:, i * 256:(i + 1) * 256])
            dhp[2 * i] = t[:, :BLK].astype(BF16)
            dhp[2 * i + 1] = t[:, BLK:].astype(BF16)
        go(h_copy(0))

    def dh_pair():
        h_copy(0).wait_recv()
        for d in (2, 1, 3):
            yb = yrel(d)
            dhs[d - 1] = (dhp[yb, khalf, :].astype(F32) + dhc[yb].astype(F32)).astype(BF16)
            go(h_copy(d))

    def dh_total():
        for d in (1, 3, 2):
            h_copy(d).wait_recv()
        t = dhp[y, khalf, :].astype(F32) + dhc[y].astype(F32)
        for j in range(3):
            t = t + dhy[j].astype(F32)
        dht[...] = t

    def transpose_tokens():
        @pl.loop(0, DW // BLK)
        def _(i):
            cs = pl.ds(pl.multiple_of(i * BLK, BLK), BLK)
            xt[cs, :] = x_all[:, cs].astype(F32).T.astype(BF16)

    def weight_grads(first, last):
        weight_grads_of(first, last)
        cs = slice(first * BLK, last * BLK)
        store(ggate_ref.at[:, cs], ggate_hbm.at[:, cs])
        store(gup_ref.at[:, cs], gup_hbm.at[:, cs])
        store(gdown_ref.at[cs], gdown_hbm.at[cs])

    def weight_grads_of(first, last):
        @pl.loop(first, last)
        def _(j):
            acc = nn(xt[...], act[j, :, :2 * BLK])
            cs = pl.ds(pl.multiple_of(j * BLK, BLK), BLK)
            for i in range(DW // BLK):
                f = flags[j, i].astype(F32)
                blk = acc[i * BLK:(i + 1) * BLK] * f
                ggate_ref[i * BLK:(i + 1) * BLK, cs] = blk[:, :BLK].astype(BF16)
                gup_ref[i * BLK:(i + 1) * BLK, cs] = blk[:, BLK:].astype(BF16)
            hidt[...] = act[j, :, 2 * BLK:].astype(F32).T.astype(BF16)
            acc = nn(hidt[...], dy[...])
            for i in range(DW // BLK):
                f = flags[j, i].astype(F32)
                gdown_ref[cs, i * BLK:(i + 1) * BLK] = (acc[:, i * BLK:(i + 1) * BLK] * f).astype(BF16)

    def make_perm():
        ocol[...] = jnp.broadcast_to(order[...].reshape(1, TOK), (BLK, TOK)).astype(F32).T
        lane = lax.broadcasted_iota(jnp.int32, (PLANE, BLK), 1).astype(F32)
        for q in range(NQ):
            for p in range(2):
                o = ocol[pl.ds(pl.multiple_of(zrel(RHO[q][p]) * PLANE, 32), PLANE), :]
                for j in range(TOK // BLK):
                    perm[rows_of(q, p), j * BLK:(j + 1) * BLK] = jnp.where(o == lane + float(j * BLK), 1.0, 0.0).astype(BF16)

    T.start()
    G.start()
    make_perm()
    T.step(1)
    G.step(1)
    for cp in loads[2:]:
        cp.wait()
    masks(0, 4)
    T.step(2)
    G.step(2)
    masks(4, 8)
    T.step(3)
    G.step(3)
    stage_p(0)
    gpair(0)
    T.step(4)
    G.step(4)
    stage_p(1)
    gpair(1)
    T.step(5)
    stage_c(0)
    stage_p(2)
    G.step(5)
    gpair(2)
    gpair(3)
    dh_partial()
    stage_c(1)
    stage_p(3)
    stage_c(2)
    dh_pair()
    stage_c(3)
    dh_total()
    stage_y(3)
    stage_y(2)
    stage_y(1)
    stage_a(3)
    stage_y(0)
    stage_a(2)
    stage_b(3)
    stage_a(1)
    stage_b(2)
    stage_a(0)
    stage_x(3)
    stage_b(1)
    stage_x(2)
    stage_b(0)
    permute()
    transpose_tokens()
    weight_grads(0, 1)
    stage_x(1)
    weight_grads(1, 2)
    stage_x(0)
    weight_grads(2, 4)
    for d in (1, 7, 2, 6, 3, 5, 4):
        rz_copy(d, zsrc.at[0, 0]).wait_recv()
    t = zsrc[0, 0].astype(F32)
    for j in range(NZ - 1):
        t = t + zrecv[j].astype(F32)
    gin_ref[...] = jnp.concatenate([t[:ROWS], t[ROWS:]], axis=1).astype(BF16)

    store(gin_ref, gin_hbm)
    for cp in started:
        cp.wait_send()
    for cp in stores:
        cp.wait()


def copy_kernel(a, b, c, d, oa, ob, oc, od, va, vb, vc, vd, lsem, ssem):
    loads, stores = [], []
    for src, mid, dst, n in ((b, vb, ob, 4), (c, vc, oc, 4), (d, vd, od, 4), (a, va, oa, 1)):
        step = src.shape[0] // n
        for i in range(n):
            rows = pl.ds(i * step, step)
            loads.append(pltpu.make_async_copy(src.at[rows], mid.at[rows], lsem.at[len(loads)]))
            stores.append(pltpu.make_async_copy(mid.at[rows], dst.at[rows], ssem.at[len(stores)]))
    for cp in loads:
        cp.start()
    for ld, st in zip(loads, stores):
        ld.wait()
        st.start()
    for cp in stores:
        cp.wait()


def on_device(tokens, grad_out, w_gate, w_up, w_down, block_flags, token_order):
    vmem = pl.BlockSpec(memory_space=pltpu.VMEM)
    smem = pl.BlockSpec(memory_space=pltpu.SMEM)
    hbm = pl.BlockSpec(memory_space=pl.ANY)
    V = pltpu.VMEM
    n = NZ * NX
    half_slab = (n, 2 * ROWS, DW // 4)
    sems = [5, 10]
    for _ in range(2):
        for m in (3, 8 * NP, 8, 24):
            sems += [m, m]
    for m in (NQ, 3 * NQ, 4, 3 * NQ, 4 * NQ, 3 * NQ, 7):
        sems += [m, m]
    scratch = [
        V((ROWS, DW), BF16), V((ROWS, DW), BF16), V((ROWS, DW), BF16),
        V((DW, FW), BF16), V((DW, FW), BF16), V((FW, DW), BF16),
        V((DW, FW), BF16), V((DW, FW), BF16), V((FW, DW), BF16),
        V((NY, DW, 2 * BLK), BF16), V((FW, DW), BF16),
        V(half_slab, BF16), V(half_slab, BF16), V(half_slab, BF16), V(half_slab, BF16),
        V((TOK, DW), BF16), V((TOK, DW), BF16), V((TOK, DW), BF16),
        V((DW, TOK), BF16), V((TOK, TOK), BF16), V((TOK, BLK), F32),
        V((NQ, NY, 2 * PLANE, 2 * BLK), BF16), V((NQ, NY, PLANE, 2 * BLK), BF16),
        V((NQ, NY - 1, PLANE, 2 * BLK), BF16), V((NQ, NY - 1, PLANE, 2 * BLK), BF16),
        V((TOK, FW), BF16), V((NY, TOK, BLK), BF16), V((NY, HALF, BLK), BF16),
        V((NY - 1, HALF, BLK), BF16), V((NY - 1, HALF, BLK), BF16), V((HALF, BLK), F32),
        V((NY, TOK, 3 * BLK), BF16), V((BLK, TOK), BF16),
        V((2, 2 * PLANE, DW), F32),
        V((NQ, NX, 2) + SLAB, BF16), V((NQ, NX - 1, 2) + SLAB, BF16),
        V((NQ, 2) + SLAB, BF16), V((NZ - 1,) + SLAB, BF16),
    ] + [pltpu.SemaphoreType.DMA((m,)) for m in sems]
    out_shape = (
        jax.ShapeDtypeStruct((ROWS, DW), BF16),
        jax.ShapeDtypeStruct((DW, FW), BF16),
        jax.ShapeDtypeStruct((DW, FW), BF16),
        jax.ShapeDtypeStruct((FW, DW), BF16),
    )
    out = pl.pallas_call(
        kernel,
        out_shape=out_shape,
        in_specs=[hbm, hbm, hbm, hbm, hbm, smem, vmem],
        out_specs=(hbm,) * 4,
        scratch_shapes=scratch,
        compiler_params=pltpu.CompilerParams(
            collective_id=0, has_side_effects=True, vmem_limit_bytes=58 * 2**20),
        name="layer_backward",
    )(tokens, grad_out, w_gate, w_up, w_down, block_flags.T, token_order)
    return pl.pallas_call(
        copy_kernel,
        out_shape=out_shape,
        in_specs=[hbm] * 4,
        out_specs=(hbm,) * 4,
        scratch_shapes=[V(o.shape, o.dtype) for o in out_shape] + [pltpu.SemaphoreType.DMA((13,))] * 2,
        compiler_params=pltpu.CompilerParams(vmem_limit_bytes=58 * 2**20),
        name="hand_over",
    )(*out)


def solution(mesh):
    return jax.shard_map(
        on_device,
        mesh=mesh,
        in_specs=(
            P("col", "row"), P("col", "row"), P("row", "col"), P("row", "col"),
            P("col", "row"), P("row", "col"), P(),
        ),
        out_specs=(P("col", "row"), P("row", "col"), P("row", "col"), P("col", "row")),
        check_vma=False,
    )
```

```python
import functools

import jax
import jax.numpy as jnp
from jax import lax
from jax.experimental import pallas as pl
from jax.experimental.pallas import tpu as pltpu
from jax.sharding import PartitionSpec as P

MESH = pl.DeviceIdType.MESH
F32 = jnp.float32
BF16 = jnp.bfloat16

NY, NK, NZ, NX = 4, 2, 8, 4
ROWS = 24
TOK = 768
HALF = TOK // 2
DW = 1024
FW = 512
BLK = 128
SLAB = (2 * ROWS, DW // 2)
PLANE = NX * ROWS
RHO = ((0, -1), (1, -2), (2, -3), (3, 4))
NQ = len(RHO)
NP = 4
SW = NX // NP


def nt(a, b):
    return lax.dot_general(a, b, (((1,), (1,)), ((), ())), preferred_element_type=F32)


def nn(a, b):
    return lax.dot_general(a, b, (((1,), (0,)), ((), ())), preferred_element_type=F32)


def kernel(tok_hbm, go_hbm, wg_hbm, wu_hbm, wd_hbm, flags, order,
           gin_hbm, ggate_hbm, gup_hbm, gdown_hbm,
           tok_ref, go_ref, gin_ref, ggate_ref, gup_ref, gdown_ref,
           raw_g, raw_u, raw_d, wgu, wgut, wd, ga, gb, ta, tb, x_all, g_all, dy, xt, perm, ocol,
           part, crecv, ssend, yrecv, dhu, dhp, dhc, dhs, dhy, dht, act, hid, hidt, dxf, rsx, xrecv, zsrc, zrecv,
           wsem, osem, gxa_s, gxa_r, gza_s, gza_r, gzb_s, gzb_r, gxb_s, gxb_r,
           txa_s, txa_r, tza_s, tza_r, tzb_s, tzb_r, txb_s, txb_r,
           c_s, c_r, y_s, y_r, h_s, h_r, a_s, a_r, b_s, b_r, rx_s, rx_r, rz_s, rz_r, e_s, e_r, f_s, f_r):
    r = lax.axis_index("row")
    c = lax.axis_index("col")
    y, k, z, x = r // 2, lax.rem(r, 2), c // 4, lax.rem(c, 4)

    def at(dy_=0, dk=0, dz=0, dx=0):
        return (lax.rem(y + dy_ + NY, NY) * 2 + lax.rem(k + dk, 2),
                lax.rem(z + dz + NZ, NZ) * 4 + lax.rem(x + dx + NX, NX))

    def zrel(d):
        return lax.rem(z + d + 2 * NZ, NZ)

    def yrel(d):
        return lax.rem(y + d + NY, NY)

    def xrel(d):
        return lax.rem(x + d + NX, NX)

    started = []

    def rc(src, dst, ss, rs, dev):
        return pltpu.make_async_remote_copy(src_ref=src, dst_ref=dst, send_sem=ss, recv_sem=rs,
                                            device_id=dev, device_id_type=MESH)

    def go(cp):
        cp.start()
        started.append(cp)


    peers = ([dict(dx=d) for d in range(1, NX)] + [dict(dz=d) for d in (1, 7, 2, 6, 3, 5, 4)]
             + [dict(dy_=d) for d in range(1, NY)] + [dict(dk=1)])
    bar = pltpu.get_barrier_semaphore()
    for p in peers:
        pl.semaphore_signal(bar, inc=1, device_id=at(**p), device_id_type=MESH)

    loads = [pltpu.make_async_copy(s, d, wsem.at[i])
             for i, (s, d) in enumerate(((go_hbm, go_ref), (tok_hbm, tok_ref),
                                         (wd_hbm, raw_d), (wg_hbm, raw_g), (wu_hbm, raw_u)))]
    for cp in loads:
        cp.start()
    stores = []

    def store(src, dst):
        cp = pltpu.make_async_copy(src, dst, osem.at[len(stores)])
        cp.start()
        stores.append(cp)

    QW = DW // 4

    def to_slabs(ref, a, b):
        v = ref[...].astype(F32)
        a[c] = jnp.concatenate([v[:, :QW], v[:, QW:2 * QW]], axis=0).astype(BF16)
        b[c] = jnp.concatenate([v[:, 2 * QW:3 * QW], v[:, 3 * QW:]], axis=0).astype(BF16)

    loads[0].wait()
    to_slabs(go_ref, ga, gb)
    loads[1].wait()
    to_slabs(tok_ref, ta, tb)
    pl.semaphore_wait(bar, len(peers))

    class Gather:
        def __init__(self, a, b, xa_s, xa_r, za_s, za_r, zb_s, zb_r, xb_s, xb_r):
            self.a, self.b = a, b
            self.xa, self.za, self.zb, self.xb = (xa_s, xa_r), (za_s, za_r), (zb_s, zb_r), (xb_s, xb_r)

        def xa_copy(self, d, src):
            ref = self.a.at[src]
            return rc(ref, ref, self.xa[0].at[d - 1], self.xa[1].at[d - 1], at(dx=d))

        def za_copy(self, direction, s, j, src_rel):
            i = ((0 if direction == 1 else 4) + s - 1) * NP + j
            ref = self.a.at[pl.ds(zrel(src_rel) * NX + j * SW, SW)]
            return rc(ref, ref, self.za[0].at[i], self.za[1].at[i], at(dz=direction))

        def zb_copy(self, direction, s, src_rel):
            i = (0 if direction == 1 else 4) + s - 1
            src = zrel(src_rel) * NX + x
            ref = self.b.at[src]
            if s == 4:
                ref = self.b.at[src, :, pl.ds(0 if direction == 1 else QW // 2, QW // 2)]
            return rc(ref, ref, self.zb[0].at[i], self.zb[1].at[i], at(dz=direction))

        def xb_copy(self, rel, d, src):
            i = (rel % NZ) * 3 + d - 1
            ref = self.b.at[src]
            return rc(ref, ref, self.xb[0].at[i], self.xb[1].at[i], at(dx=d))

        def xb_send(self, rel):
            for d in (2, 1, 3):
                go(self.xb_copy(rel, d, zrel(rel) * NX + x))

        def xb_wait(self, rel):
            for d in (1, 3, 2):
                self.xb_copy(rel, d, zrel(rel) * NX + xrel(-d)).wait_recv()

        def start(self):
            for d in (2, 1, 3):
                go(self.xa_copy(d, c))
            go(self.zb_copy(1, 1, 0))
            go(self.zb_copy(-1, 1, 0))
            self.xb_send(0)

        def step(self, t, fill=()):
            fill = list(fill)

            def work():
                if fill:
                    fill.pop(0)()

            if t <= 4:
                for direction in (1, -1):
                    self.zb_copy(direction, t, -direction * t).wait_recv()
                    if t < 4:
                        go(self.zb_copy(direction, t + 1, -direction * t))
                        self.xb_send(-direction * t)
                    work()
                if t == 4:
                    self.xb_send(4)
            if t == 1:
                for d in (1, 3, 2):
                    self.xa_copy(d, z * NX + xrel(-d)).wait_recv()
                for j in range(NP):
                    for direction in (1, -1):
                        go(self.za_copy(direction, 1, j, 0))
                while fill:
                    work()
                return
            s = t - 1
            for j in range(NP):
                for direction in (1, -1):
                    mine = (j < NP // 2) == (direction == 1)
                    if s < 4 or mine:
                        self.za_copy(direction, s, j, -direction * s).wait_recv()
                    if s < 3 or (s == 3 and mine):
                        go(self.za_copy(direction, s + 1, j, -direction * s))
                work()
            while fill:
                work()

    G = Gather(ga, gb, gxa_s, gxa_r, gza_s, gza_r, gzb_s, gzb_r, gxb_s, gxb_r)
    T = Gather(ta, tb, txa_s, txa_r, tza_s, tza_r, tzb_s, tzb_r, txb_s, txb_r)

    def masks(i0, i1):
        @pl.loop(i0, i1)
        def _(i):
            rows = pl.ds(pl.multiple_of(i * BLK, BLK), BLK)
            for j in range(FW // BLK):
                f = flags[j, i].astype(F32)
                cs = slice(j * BLK, (j + 1) * BLK)
                wgu[j, rows, :BLK] = (raw_g[rows, cs].astype(F32) * f).astype(BF16)
                wgu[j, rows, BLK:] = (raw_u[rows, cs].astype(F32) * f).astype(BF16)
                wd[cs, rows] = (raw_d[cs, rows].astype(F32) * f).astype(BF16)

    def unslab(a, b, c0, dst, row0):
        rows = pl.ds(row0, 2 * ROWS)
        for n, buf in enumerate((a, b)):
            v, w = buf[c0].astype(F32), buf[c0 + 1].astype(F32)
            dst[rows, 2 * n * QW:(2 * n + 1) * QW] = jnp.concatenate([v[:ROWS], w[:ROWS]], axis=0).astype(BF16)
            dst[rows, (2 * n + 1) * QW:(2 * n + 2) * QW] = jnp.concatenate([v[ROWS:], w[ROWS:]], axis=0).astype(BF16)

    def rows_of(q, p):
        return slice(p * HALF + q * PLANE, p * HALF + (q + 1) * PLANE)

    def krows(q):
        return pl.ds(pl.multiple_of(k * HALF + q * PLANE, 32), PLANE)

    kplane = pl.ds(pl.multiple_of(k * PLANE, 32), PLANE)
    khalf = pl.ds(pl.multiple_of(k * HALF, HALF), HALF)

    def c_copy(q):
        sib = pl.ds(pl.multiple_of((1 - k) * PLANE, 32), PLANE)
        return rc(part.at[q, :, sib], crecv.at[q], c_s.at[q], c_r.at[q], at(dk=1))

    def pieces_p(q):
        def rows(p):
            plane = zrel(RHO[q][p])
            T.xb_wait(RHO[q][p])
            for xx in (0, 2):
                unslab(ta, tb, plane * NX + xx, x_all, p * HALF + q * PLANE + xx * ROWS)

        def product(d):
            lhs = jnp.concatenate([x_all[rows_of(q, 0), :], x_all[rows_of(q, 1), :]], axis=0)
            part[q, d] = nn(lhs, wgu[yrel(d)]).astype(BF16)
            if d == NY - 1:
                go(c_copy(q))

        return ([functools.partial(rows, p) for p in range(2)]
                + [functools.partial(product, d) for d in range(NY)])

    def stage_p(q):
        for piece in pieces_p(q):
            piece()

    def y_copy(q, d):
        i = q * 3 + d - 1
        return rc(ssend.at[q, d - 1], yrecv.at[q, d - 1], y_s.at[i], y_r.at[i], at(dy_=d))

    def stage_c(q):
        c_copy(q).wait_recv()
        for d in (2, 1, 3):
            ssend[q, d - 1] = (part[q, d, kplane, :].astype(F32) + crecv[q, d].astype(F32)).astype(BF16)
            go(y_copy(q, d))

    def a_copy(q, d, src):
        i = q * 3 + d - 1
        ref = act.at[krows(q), pl.ds(pl.multiple_of(src * 256, 256), 256)]
        return rc(ref, ref, a_s.at[i], a_r.at[i], at(dy_=d))

    def b_copy(q, d, src, half):
        i = q * 4 + d
        ref = act.at[pl.ds(pl.multiple_of(half * HALF + q * PLANE, 32), PLANE), pl.ds(pl.multiple_of(src * 256, 256), 256)]
        return rc(ref, ref, b_s.at[i], b_r.at[i], at(dk=1))

    def stage_y(q):
        for d in (1, 3, 2):
            y_copy(q, d).wait_recv()
        t = part[q, 0, kplane, :].astype(F32) + crecv[q, 0].astype(F32)
        for j in range(3):
            t = t + yrecv[q, j].astype(F32)
        gate, up = t[:, :BLK], t[:, BLK:]
        dh = dht[q * PLANE:(q + 1) * PLANE, :]
        sig = 1.0 / (1.0 + jnp.exp(-gate))
        silu = gate * sig
        rows = krows(q)
        act[rows, pl.ds(pl.multiple_of(y * 256, 256), BLK)] = (dh * up * sig * (1.0 + gate * (1.0 - sig))).astype(BF16)
        act[rows, pl.ds(pl.multiple_of(y * 256 + BLK, BLK), BLK)] = (dh * silu).astype(BF16)
        hid[y, rows, :] = (silu * up).astype(BF16)
        for d in (2, 1, 3):
            go(a_copy(q, d, y))
        go(b_copy(q, 0, y, k))

    def e_copy(d, src):
        ref = hid.at[src, khalf]
        return rc(ref, ref, e_s.at[d - 1], e_r.at[d - 1], at(dy_=d))

    def f_copy(d, half):
        ref = hid.at[yrel(-d), pl.ds(pl.multiple_of(half * HALF, HALF), HALF)]
        return rc(ref, ref, f_s.at[d], f_r.at[d], at(dk=1))

    def stage_e():
        for d in (2, 1, 3):
            go(e_copy(d, y))
        go(f_copy(0, k))

    def stage_f():
        for d in (1, 3, 2):
            e_copy(d, yrel(-d)).wait_recv()
            go(f_copy(d, k))

    def stage_k():
        for d in (0, 1, 3, 2):
            f_copy(d, 1 - k).wait_recv()

    def stage_a(q):
        for d in (1, 3, 2):
            a_copy(q, d, yrel(-d)).wait_recv()
            go(b_copy(q, d, yrel(-d), k))

    def rx_copy(q, d):
        i = q * 3 + d - 1
        return rc(rsx.at[q, xrel(d)], xrecv.at[q, d - 1], rx_s.at[i], rx_r.at[i], at(dx=d))

    def stage_b(q):
        for d in (0, 1, 3, 2):
            b_copy(q, d, yrel(-d), 1 - k).wait_recv()

        lhs = jnp.concatenate([act[rows_of(q, 0), :], act[rows_of(q, 1), :]], axis=0)

        @pl.loop(0, DW // 256)
        def _(i):
            cs = pl.ds(pl.multiple_of(i * 256, 256), 256)
            dxf[q % 2, :, cs] = nn(lhs, wgut[:, cs])

        for p in range(2):
            for xx in range(NX):
                v = dxf[q % 2, p * PLANE + xx * ROWS:p * PLANE + (xx + 1) * ROWS, :]
                rsx[q, xx, p] = jnp.concatenate([v[:, :DW // 2], v[:, DW // 2:]], axis=0).astype(BF16)
        for d in (2, 1, 3):
            go(rx_copy(q, d))

    def rz_copy(rho, src):
        i = rho % NZ - 1
        return rc(src, zrecv.at[i], rz_s.at[i], rz_r.at[i], at(dz=rho))

    def stage_x(q):
        for d in (1, 3, 2):
            rx_copy(q, d).wait_recv()
        for p in range(2):
            t = rsx[q, x, p].astype(F32)
            for j in range(3):
                t = t + xrecv[q, j, p].astype(F32)
            zsrc[q, p] = t.astype(BF16)
            if RHO[q][p] != 0:
                go(rz_copy(RHO[q][p], zsrc.at[q, p]))

    def h_copy(d):
        if d == 0:
            sib = pl.ds(pl.multiple_of((1 - k) * HALF, HALF), HALF)
            return rc(dhp.at[:, sib], dhc, h_s.at[0], h_r.at[0], at(dk=1))
        return rc(dhs.at[d - 1], dhy.at[d - 1], h_s.at[d], h_r.at[d], at(dy_=d))

    def pieces_g(q):
        parts = [pl.ds(pl.multiple_of(zrel(RHO[q][p]) * PLANE, 32), PLANE) for p in range(2)]

        def rows(p):
            plane = zrel(RHO[q][p])
            G.xb_wait(RHO[q][p])
            for xx in (0, 2):
                unslab(ga, gb, plane * NX + xx, g_all, pl.multiple_of(plane * PLANE + xx * ROWS, 2 * ROWS))

        def product(i):
            lhs = jnp.concatenate([g_all[parts[0], :], g_all[parts[1], :]], axis=0)
            t = nt(lhs, wd[i * 256:(i + 1) * 256, :]).astype(BF16)
            dhu[parts[0], i * 256:(i + 1) * 256] = t[:PLANE]
            dhu[parts[1], i * 256:(i + 1) * 256] = t[PLANE:]

        return ([functools.partial(rows, p) for p in range(2)]
                + [functools.partial(product, i) for i in range(2)])

    def gpair(q):
        for piece in pieces_g(q):
            piece()

    def permute():
        @pl.loop(0, DW // 256)
        def _(i):
            cs = pl.ds(pl.multiple_of(i * 256, 256), 256)
            dy[:, cs] = nn(perm[...], g_all[:, cs]).astype(BF16)

    def dh_partial():
        for i in range(2):
            t = nn(perm[...], dhu[:, i * 256:(i + 1) * 256])
            dhp[2 * i] = t[:, :BLK].astype(BF16)
            dhp[2 * i + 1] = t[:, BLK:].astype(BF16)
        go(h_copy(0))

    def dh_pair():
        h_copy(0).wait_recv()
        for d in (2, 1, 3):
            yb = yrel(d)
            dhs[d - 1] = (dhp[yb, khalf, :].astype(F32) + dhc[yb].astype(F32)).astype(BF16)
            go(h_copy(d))

    def dh_total():
        for d in (1, 3, 2):
            h_copy(d).wait_recv()
        t = dhp[y, khalf, :].astype(F32) + dhc[y].astype(F32)
        for j in range(3):
            t = t + dhy[j].astype(F32)
        dht[...] = t

    def transpose_tokens():
        @pl.loop(0, DW // BLK)
        def _(i):
            cs = pl.ds(pl.multiple_of(i * BLK, BLK), BLK)
            xt[cs, :] = x_all[:, cs].astype(F32).T.astype(BF16)

    def weight_grads(first, last):
        @pl.loop(first, last)
        def _(j):
            acc = nn(xt[...], act[:, pl.ds(pl.multiple_of(j * 256, 256), 256)])
            cs = pl.ds(pl.multiple_of(j * BLK, BLK), BLK)
            for i in range(DW // BLK):
                f = flags[j, i].astype(F32)
                blk = acc[i * BLK:(i + 1) * BLK] * f
                ggate_ref[i * BLK:(i + 1) * BLK, cs] = blk[:, :BLK].astype(BF16)
                gup_ref[i * BLK:(i + 1) * BLK, cs] = blk[:, BLK:].astype(BF16)

        cs = slice(first * BLK, last * BLK)
        store(ggate_ref.at[:, cs], ggate_hbm.at[:, cs])
        store(gup_ref.at[:, cs], gup_hbm.at[:, cs])

    def down_grads(first, last):
        @pl.loop(first, last)
        def _(j):
            hidt[...] = hid[j].astype(F32).T.astype(BF16)
            acc = nn(hidt[...], dy[...])
            cs = pl.ds(pl.multiple_of(j * BLK, BLK), BLK)
            for i in range(DW // BLK):
                f = flags[j, i].astype(F32)
                gdown_ref[cs, i * BLK:(i + 1) * BLK] = (acc[:, i * BLK:(i + 1) * BLK] * f).astype(BF16)

        cs = slice(first * BLK, last * BLK)
        store(gdown_ref.at[cs], gdown_hbm.at[cs])

    def pieces_perm():
        def column():
            ocol[...] = jnp.broadcast_to(order[...].reshape(1, TOK), (BLK, TOK)).astype(F32).T

        def block(q, p):
            lane = lax.broadcasted_iota(jnp.int32, (PLANE, BLK), 1).astype(F32)
            o = ocol[pl.ds(pl.multiple_of(zrel(RHO[q][p]) * PLANE, 32), PLANE), :]
            for j in range(TOK // BLK):
                perm[rows_of(q, p), j * BLK:(j + 1) * BLK] = jnp.where(o == lane + float(j * BLK), 1.0, 0.0).astype(BF16)

        return [column] + [functools.partial(block, q, p) for q in range(NQ) for p in range(2)]

    def pieces_transpose():
        def one(j):
            wgut[j * 256:(j + 1) * 256, :] = wgu[j].astype(F32).T.astype(BF16)

        return [functools.partial(one, j) for j in range(NY)]

    def make_perm():
        for piece in pieces_perm():
            piece()

    def pieces_masks():
        def wait():
            for cp in loads[2:]:
                cp.wait()

        return [wait] + [functools.partial(masks, i, i + 1) for i in range(DW // BLK)]

    T.start()
    G.start()
    T.step(1, pieces_masks()[:4])
    G.step(1, pieces_masks()[4:])
    T.step(2, pieces_perm()[:5])
    G.step(2, pieces_perm()[5:])
    T.step(3, pieces_transpose())
    G.step(3, pieces_p(0))
    T.step(4, pieces_g(0))
    stage_c(0)
    G.step(4, pieces_p(1))
    T.step(5, pieces_g(1))
    stage_c(1)
    G.step(5, pieces_p(2))
    gpair(2)
    gpair(3)
    dh_partial()
    stage_p(3)
    stage_c(2)
    dh_pair()
    stage_c(3)
    permute()
    transpose_tokens()
    dh_total()
    stage_y(2)
    stage_y(1)
    stage_a(2)
    stage_y(3)
    stage_a(1)
    stage_b(2)
    stage_y(0)
    stage_e()
    stage_a(3)
    stage_b(1)
    stage_a(0)
    stage_b(3)
    stage_x(2)
    stage_b(0)
    stage_x(1)
    stage_f()
    stage_x(3)
    weight_grads(0, 2)
    stage_k()
    down_grads(0, 1)
    stage_x(0)
    weight_grads(2, 4)
    down_grads(1, 4)
    for d in (1, 7, 2, 6, 3, 5, 4):
        rz_copy(d, zsrc.at[0, 0]).wait_recv()
    t = zsrc[0, 0].astype(F32)
    for j in range(NZ - 1):
        t = t + zrecv[j].astype(F32)
    gin_ref[...] = jnp.concatenate([t[:ROWS], t[ROWS:]], axis=1).astype(BF16)

    store(gin_ref, gin_hbm)
    for cp in started:
        cp.wait_send()
    for cp in stores:
        cp.wait()


def copy_kernel(a, b, c, d, oa, ob, oc, od, va, vb, vc, vd, lsem, ssem):
    loads, stores = [], []
    for src, mid, dst, n in ((b, vb, ob, 4), (c, vc, oc, 4), (d, vd, od, 4), (a, va, oa, 1)):
        step = src.shape[0] // n
        for i in range(n):
            rows = pl.ds(i * step, step)
            loads.append(pltpu.make_async_copy(src.at[rows], mid.at[rows], lsem.at[len(loads)]))
            stores.append(pltpu.make_async_copy(mid.at[rows], dst.at[rows], ssem.at[len(stores)]))
    for cp in loads:
        cp.start()
    for ld, st in zip(loads, stores):
        ld.wait()
        st.start()
    for cp in stores:
        cp.wait()


def on_device(tokens, grad_out, w_gate, w_up, w_down, block_flags, token_order):
    vmem = pl.BlockSpec(memory_space=pltpu.VMEM)
    smem = pl.BlockSpec(memory_space=pltpu.SMEM)
    hbm = pl.BlockSpec(memory_space=pl.ANY)
    V = pltpu.VMEM
    n = NZ * NX
    half_slab = (n, 2 * ROWS, DW // 4)
    sems = [5, 16]
    for _ in range(2):
        for m in (3, 8 * NP, 8, 24):
            sems += [m, m]
    for m in (NQ, 3 * NQ, 4, 3 * NQ, 4 * NQ, 3 * NQ, 7, 3, 4):
        sems += [m, m]
    scratch = [
        V((ROWS, DW), BF16), V((ROWS, DW), BF16), V((ROWS, DW), BF16),
        V((DW, FW), BF16), V((DW, FW), BF16), V((FW, DW), BF16),
        V((DW, FW), BF16), V((DW, FW), BF16), V((FW, DW), BF16),
        V((NY, DW, 2 * BLK), BF16), V((2 * FW, DW), BF16), V((FW, DW), BF16),
        V(half_slab, BF16), V(half_slab, BF16), V(half_slab, BF16), V(half_slab, BF16),
        V((TOK, DW), BF16), V((TOK, DW), BF16), V((TOK, DW), BF16),
        V((DW, TOK), BF16), V((TOK, TOK), BF16), V((TOK, BLK), F32),
        V((NQ, NY, 2 * PLANE, 2 * BLK), BF16), V((NQ, NY, PLANE, 2 * BLK), BF16),
        V((NQ, NY - 1, PLANE, 2 * BLK), BF16), V((NQ, NY - 1, PLANE, 2 * BLK), BF16),
        V((TOK, FW), BF16), V((NY, TOK, BLK), BF16), V((NY, HALF, BLK), BF16),
        V((NY - 1, HALF, BLK), BF16), V((NY - 1, HALF, BLK), BF16), V((HALF, BLK), F32),
        V((TOK, 2 * FW), BF16), V((NY, TOK, BLK), BF16), V((BLK, TOK), BF16),
        V((2, 2 * PLANE, DW), F32),
        V((NQ, NX, 2) + SLAB, BF16), V((NQ, NX - 1, 2) + SLAB, BF16),
        V((NQ, 2) + SLAB, BF16), V((NZ - 1,) + SLAB, BF16),
    ] + [pltpu.SemaphoreType.DMA((m,)) for m in sems]
    out_shape = (
        jax.ShapeDtypeStruct((ROWS, DW), BF16),
        jax.ShapeDtypeStruct((DW, FW), BF16),
        jax.ShapeDtypeStruct((DW, FW), BF16),
        jax.ShapeDtypeStruct((FW, DW), BF16),
    )
    out = pl.pallas_call(
        kernel,
        out_shape=out_shape,
        in_specs=[hbm, hbm, hbm, hbm, hbm, smem, vmem],
        out_specs=(hbm,) * 4,
        scratch_shapes=scratch,
        compiler_params=pltpu.CompilerParams(
            collective_id=0, has_side_effects=True, vmem_limit_bytes=58 * 2**20),
        name="layer_backward",
    )(tokens, grad_out, w_gate, w_up, w_down, block_flags.T, token_order)
    return pl.pallas_call(
        copy_kernel,
        out_shape=out_shape,
        in_specs=[hbm] * 4,
        out_specs=(hbm,) * 4,
        scratch_shapes=[V(o.shape, o.dtype) for o in out_shape] + [pltpu.SemaphoreType.DMA((13,))] * 2,
        compiler_params=pltpu.CompilerParams(vmem_limit_bytes=58 * 2**20),
        name="hand_over",
    )(*out)


def solution(mesh):
    return jax.shard_map(
        on_device,
        mesh=mesh,
        in_specs=(
            P("col", "row"), P("col", "row"), P("row", "col"), P("row", "col"),
            P("col", "row"), P("row", "col"), P(),
        ),
        out_specs=(P("col", "row"), P("row", "col"), P("row", "col"), P("col", "row")),
        check_vma=False,
    )
```

```python
import functools

import jax
import jax.numpy as jnp
from jax import lax
from jax.experimental import pallas as pl
from jax.experimental.pallas import tpu as pltpu
from jax.sharding import PartitionSpec as P

MESH = pl.DeviceIdType.MESH
F32 = jnp.float32
BF16 = jnp.bfloat16

NY, NK, NZ, NX = 4, 2, 8, 4
ROWS = 24
TOK = 768
HALF = TOK // 2
DW = 1024
FW = 512
BLK = 128
SLAB = (2 * ROWS, DW // 2)
PLANE = NX * ROWS
RHO = ((0, -1), (1, -2), (2, -3), (3, 4))
NQ = len(RHO)
NP = 4
SW = NX // NP


def nt(a, b):
    return lax.dot_general(a, b, (((1,), (1,)), ((), ())), preferred_element_type=F32)


def nn(a, b):
    return lax.dot_general(a, b, (((1,), (0,)), ((), ())), preferred_element_type=F32)


def kernel(tok_hbm, go_hbm, wg_hbm, wu_hbm, wd_hbm, flags, order,
           gin_ref, ggate_ref, gup_ref, gdown_ref,
           tok_ref, go_ref,
           raw_g, raw_u, raw_d, wgu, wgut, wd, ga, gb, ta, tb, x_all, g_all, dy, xt, perm, ocol,
           part, crecv, ssend, yrecv, dhu, dhp, dhc, dhs, dhy, dht, act, hid, hidt, dxf, rsx, xrecv, zsrc, zrecv,
           wsem, gxa_s, gxa_r, gza_s, gza_r, gzb_s, gzb_r, gxb_s, gxb_r,
           txa_s, txa_r, tza_s, tza_r, tzb_s, tzb_r, txb_s, txb_r,
           c_s, c_r, y_s, y_r, h_s, h_r, a_s, a_r, b_s, b_r, rx_s, rx_r, rz_s, rz_r, e_s, e_r, f_s, f_r):
    r = lax.axis_index("row")
    c = lax.axis_index("col")
    y, k, z, x = r // 2, lax.rem(r, 2), c // 4, lax.rem(c, 4)

    def at(dy_=0, dk=0, dz=0, dx=0):
        return (lax.rem(y + dy_ + NY, NY) * 2 + lax.rem(k + dk, 2),
                lax.rem(z + dz + NZ, NZ) * 4 + lax.rem(x + dx + NX, NX))

    def zrel(d):
        return lax.rem(z + d + 2 * NZ, NZ)

    def yrel(d):
        return lax.rem(y + d + NY, NY)

    def xrel(d):
        return lax.rem(x + d + NX, NX)

    started = []

    def rc(src, dst, ss, rs, dev):
        return pltpu.make_async_remote_copy(src_ref=src, dst_ref=dst, send_sem=ss, recv_sem=rs,
                                            device_id=dev, device_id_type=MESH)

    def go(cp):
        cp.start()
        started.append(cp)


    peers = ([dict(dx=d) for d in range(1, NX)] + [dict(dz=d) for d in (1, 7, 2, 6, 3, 5, 4)]
             + [dict(dy_=d) for d in range(1, NY)] + [dict(dk=1)])
    bar = pltpu.get_barrier_semaphore()
    for p in peers:
        pl.semaphore_signal(bar, inc=1, device_id=at(**p), device_id_type=MESH)

    loads = [pltpu.make_async_copy(s, d, wsem.at[i])
             for i, (s, d) in enumerate(((go_hbm, go_ref), (tok_hbm, tok_ref),
                                         (wd_hbm, raw_d), (wg_hbm, raw_g), (wu_hbm, raw_u)))]
    for cp in loads:
        cp.start()
    QW = DW // 4

    def to_slabs(ref, a, b):
        v = ref[...].astype(F32)
        a[c] = jnp.concatenate([v[:, :QW], v[:, QW:2 * QW]], axis=0).astype(BF16)
        b[c] = jnp.concatenate([v[:, 2 * QW:3 * QW], v[:, 3 * QW:]], axis=0).astype(BF16)

    loads[0].wait()
    to_slabs(go_ref, ga, gb)
    loads[1].wait()
    to_slabs(tok_ref, ta, tb)
    pl.semaphore_wait(bar, len(peers))

    class Gather:
        def __init__(self, a, b, xa_s, xa_r, za_s, za_r, zb_s, zb_r, xb_s, xb_r):
            self.a, self.b = a, b
            self.xa, self.za, self.zb, self.xb = (xa_s, xa_r), (za_s, za_r), (zb_s, zb_r), (xb_s, xb_r)

        def xa_copy(self, d, src):
            ref = self.a.at[src]
            return rc(ref, ref, self.xa[0].at[d - 1], self.xa[1].at[d - 1], at(dx=d))

        def za_copy(self, direction, s, j, src_rel):
            i = ((0 if direction == 1 else 4) + s - 1) * NP + j
            ref = self.a.at[pl.ds(zrel(src_rel) * NX + j * SW, SW)]
            return rc(ref, ref, self.za[0].at[i], self.za[1].at[i], at(dz=direction))

        def zb_copy(self, direction, s, src_rel):
            i = (0 if direction == 1 else 4) + s - 1
            src = zrel(src_rel) * NX + x
            ref = self.b.at[src]
            if s == 4:
                ref = self.b.at[src, :, pl.ds(0 if direction == 1 else QW // 2, QW // 2)]
            return rc(ref, ref, self.zb[0].at[i], self.zb[1].at[i], at(dz=direction))

        def xb_copy(self, rel, d, src):
            i = (rel % NZ) * 3 + d - 1
            ref = self.b.at[src]
            return rc(ref, ref, self.xb[0].at[i], self.xb[1].at[i], at(dx=d))

        def xb_send(self, rel):
            for d in (2, 1, 3):
                go(self.xb_copy(rel, d, zrel(rel) * NX + x))

        def xb_wait(self, rel):
            for d in (1, 3, 2):
                self.xb_copy(rel, d, zrel(rel) * NX + xrel(-d)).wait_recv()

        def start(self):
            for d in (2, 1, 3):
                go(self.xa_copy(d, c))
            go(self.zb_copy(1, 1, 0))
            go(self.zb_copy(-1, 1, 0))
            self.xb_send(0)

        def step(self, t, fill=()):
            fill = list(fill)

            def work():
                if fill:
                    fill.pop(0)()

            if t <= 4:
                for direction in (1, -1):
                    self.zb_copy(direction, t, -direction * t).wait_recv()
                    if t < 4:
                        go(self.zb_copy(direction, t + 1, -direction * t))
                        self.xb_send(-direction * t)
                    work()
                if t == 4:
                    self.xb_send(4)
            if t == 1:
                for d in (1, 3, 2):
                    self.xa_copy(d, z * NX + xrel(-d)).wait_recv()
                for j in range(NP):
                    for direction in (1, -1):
                        go(self.za_copy(direction, 1, j, 0))
                while fill:
                    work()
                return
            s = t - 1
            for j in range(NP):
                for direction in (1, -1):
                    mine = (j < NP // 2) == (direction == 1)
                    if s < 4 or mine:
                        self.za_copy(direction, s, j, -direction * s).wait_recv()
                    if s < 3 or (s == 3 and mine):
                        go(self.za_copy(direction, s + 1, j, -direction * s))
                work()
            while fill:
                work()

    G = Gather(ga, gb, gxa_s, gxa_r, gza_s, gza_r, gzb_s, gzb_r, gxb_s, gxb_r)
    T = Gather(ta, tb, txa_s, txa_r, tza_s, tza_r, tzb_s, tzb_r, txb_s, txb_r)

    def masks(i0, i1):
        @pl.loop(i0, i1)
        def _(i):
            rows = pl.ds(pl.multiple_of(i * BLK, BLK), BLK)
            for j in range(FW // BLK):
                f = flags[j, i].astype(F32)
                cs = slice(j * BLK, (j + 1) * BLK)
                wgu[j, rows, :BLK] = (raw_g[rows, cs].astype(F32) * f).astype(BF16)
                wgu[j, rows, BLK:] = (raw_u[rows, cs].astype(F32) * f).astype(BF16)
                wd[cs, rows] = (raw_d[cs, rows].astype(F32) * f).astype(BF16)

    def unslab(a, b, c0, dst, row0):
        rows = pl.ds(row0, 2 * ROWS)
        for n, buf in enumerate((a, b)):
            v, w = buf[c0].astype(F32), buf[c0 + 1].astype(F32)
            dst[rows, 2 * n * QW:(2 * n + 1) * QW] = jnp.concatenate([v[:ROWS], w[:ROWS]], axis=0).astype(BF16)
            dst[rows, (2 * n + 1) * QW:(2 * n + 2) * QW] = jnp.concatenate([v[ROWS:], w[ROWS:]], axis=0).astype(BF16)

    def rows_of(q, p):
        return slice(p * HALF + q * PLANE, p * HALF + (q + 1) * PLANE)

    def krows(q):
        return pl.ds(pl.multiple_of(k * HALF + q * PLANE, 32), PLANE)

    kplane = pl.ds(pl.multiple_of(k * PLANE, 32), PLANE)
    khalf = pl.ds(pl.multiple_of(k * HALF, HALF), HALF)

    def c_copy(q):
        sib = pl.ds(pl.multiple_of((1 - k) * PLANE, 32), PLANE)
        return rc(part.at[q, :, sib], crecv.at[q], c_s.at[q], c_r.at[q], at(dk=1))

    def pieces_p(q):
        def rows(p):
            plane = zrel(RHO[q][p])
            T.xb_wait(RHO[q][p])
            for xx in (0, 2):
                unslab(ta, tb, plane * NX + xx, x_all, p * HALF + q * PLANE + xx * ROWS)

        def product(d):
            lhs = jnp.concatenate([x_all[rows_of(q, 0), :], x_all[rows_of(q, 1), :]], axis=0)
            part[q, d] = nn(lhs, wgu[yrel(d)]).astype(BF16)
            if d == NY - 1:
                go(c_copy(q))

        return ([functools.partial(rows, p) for p in range(2)]
                + [functools.partial(product, d) for d in range(NY)])

    def stage_p(q):
        for piece in pieces_p(q):
            piece()

    def y_copy(q, d):
        i = q * 3 + d - 1
        return rc(ssend.at[q, d - 1], yrecv.at[q, d - 1], y_s.at[i], y_r.at[i], at(dy_=d))

    def stage_c(q):
        c_copy(q).wait_recv()
        for d in (2, 1, 3):
            ssend[q, d - 1] = (part[q, d, kplane, :].astype(F32) + crecv[q, d].astype(F32)).astype(BF16)
            go(y_copy(q, d))

    def a_copy(q, d, src):
        i = q * 3 + d - 1
        ref = act.at[krows(q), pl.ds(pl.multiple_of(src * 256, 256), 256)]
        return rc(ref, ref, a_s.at[i], a_r.at[i], at(dy_=d))

    def b_copy(q, d, src, half):
        i = q * 4 + d
        ref = act.at[pl.ds(pl.multiple_of(half * HALF + q * PLANE, 32), PLANE), pl.ds(pl.multiple_of(src * 256, 256), 256)]
        return rc(ref, ref, b_s.at[i], b_r.at[i], at(dk=1))

    def stage_y(q):
        for d in (1, 3, 2):
            y_copy(q, d).wait_recv()
        t = part[q, 0, kplane, :].astype(F32) + crecv[q, 0].astype(F32)
        for j in range(3):
            t = t + yrecv[q, j].astype(F32)
        gate, up = t[:, :BLK], t[:, BLK:]
        dh = dht[q * PLANE:(q + 1) * PLANE, :]
        sig = 1.0 / (1.0 + jnp.exp(-gate))
        silu = gate * sig
        rows = krows(q)
        act[rows, pl.ds(pl.multiple_of(y * 256, 256), BLK)] = (dh * up * sig * (1.0 + gate * (1.0 - sig))).astype(BF16)
        act[rows, pl.ds(pl.multiple_of(y * 256 + BLK, BLK), BLK)] = (dh * silu).astype(BF16)
        hid[y, rows, :] = (silu * up).astype(BF16)
        for d in (2, 1, 3):
            go(a_copy(q, d, y))
        go(b_copy(q, 0, y, k))

    def e_copy(d, src):
        ref = hid.at[src, khalf]
        return rc(ref, ref, e_s.at[d - 1], e_r.at[d - 1], at(dy_=d))

    def f_copy(d, half):
        ref = hid.at[yrel(-d), pl.ds(pl.multiple_of(half * HALF, HALF), HALF)]
        return rc(ref, ref, f_s.at[d], f_r.at[d], at(dk=1))

    def stage_e():
        for d in (2, 1, 3):
            go(e_copy(d, y))
        go(f_copy(0, k))

    def stage_f():
        for d in (1, 3, 2):
            e_copy(d, yrel(-d)).wait_recv()
            go(f_copy(d, k))

    def stage_k():
        for d in (0, 1, 3, 2):
            f_copy(d, 1 - k).wait_recv()

    def stage_a(q):
        for d in (1, 3, 2):
            a_copy(q, d, yrel(-d)).wait_recv()
            go(b_copy(q, d, yrel(-d), k))

    def rx_copy(q, d):
        i = q * 3 + d - 1
        return rc(rsx.at[q, xrel(d)], xrecv.at[q, d - 1], rx_s.at[i], rx_r.at[i], at(dx=d))

    def stage_b(q):
        for d in (0, 1, 3, 2):
            b_copy(q, d, yrel(-d), 1 - k).wait_recv()

        lhs = jnp.concatenate([act[rows_of(q, 0), :], act[rows_of(q, 1), :]], axis=0)

        @pl.loop(0, DW // 256)
        def _(i):
            cs = pl.ds(pl.multiple_of(i * 256, 256), 256)
            dxf[q % 2, :, cs] = nn(lhs, wgut[:, cs])

        for p in range(2):
            for xx in range(NX):
                v = dxf[q % 2, p * PLANE + xx * ROWS:p * PLANE + (xx + 1) * ROWS, :]
                rsx[q, xx, p] = jnp.concatenate([v[:, :DW // 2], v[:, DW // 2:]], axis=0).astype(BF16)
        for d in (2, 1, 3):
            go(rx_copy(q, d))

    def rz_copy(rho, src):
        i = rho % NZ - 1
        return rc(src, zrecv.at[i], rz_s.at[i], rz_r.at[i], at(dz=rho))

    def stage_x(q):
        for d in (1, 3, 2):
            rx_copy(q, d).wait_recv()
        for p in range(2):
            t = rsx[q, x, p].astype(F32)
            for j in range(3):
                t = t + xrecv[q, j, p].astype(F32)
            zsrc[q, p] = t.astype(BF16)
            if RHO[q][p] != 0:
                go(rz_copy(RHO[q][p], zsrc.at[q, p]))

    def h_copy(d):
        if d == 0:
            sib = pl.ds(pl.multiple_of((1 - k) * HALF, HALF), HALF)
            return rc(dhp.at[:, sib], dhc, h_s.at[0], h_r.at[0], at(dk=1))
        return rc(dhs.at[d - 1], dhy.at[d - 1], h_s.at[d], h_r.at[d], at(dy_=d))

    def pieces_g(q):
        parts = [pl.ds(pl.multiple_of(zrel(RHO[q][p]) * PLANE, 32), PLANE) for p in range(2)]

        def rows(p):
            plane = zrel(RHO[q][p])
            G.xb_wait(RHO[q][p])
            for xx in (0, 2):
                unslab(ga, gb, plane * NX + xx, g_all, pl.multiple_of(plane * PLANE + xx * ROWS, 2 * ROWS))

        def product(i):
            lhs = jnp.concatenate([g_all[parts[0], :], g_all[parts[1], :]], axis=0)
            t = nt(lhs, wd[i * 256:(i + 1) * 256, :]).astype(BF16)
            dhu[parts[0], i * 256:(i + 1) * 256] = t[:PLANE]
            dhu[parts[1], i * 256:(i + 1) * 256] = t[PLANE:]

        return ([functools.partial(rows, p) for p in range(2)]
                + [functools.partial(product, i) for i in range(2)])

    def gpair(q):
        for piece in pieces_g(q):
            piece()

    def permute():
        @pl.loop(0, DW // 256)
        def _(i):
            cs = pl.ds(pl.multiple_of(i * 256, 256), 256)
            dy[:, cs] = nn(perm[...], g_all[:, cs]).astype(BF16)

    def dh_partial():
        for i in range(2):
            t = nn(perm[...], dhu[:, i * 256:(i + 1) * 256])
            dhp[2 * i] = t[:, :BLK].astype(BF16)
            dhp[2 * i + 1] = t[:, BLK:].astype(BF16)
        go(h_copy(0))

    def dh_pair():
        h_copy(0).wait_recv()
        for d in (2, 1, 3):
            yb = yrel(d)
            dhs[d - 1] = (dhp[yb, khalf, :].astype(F32) + dhc[yb].astype(F32)).astype(BF16)
            go(h_copy(d))

    def dh_total():
        for d in (1, 3, 2):
            h_copy(d).wait_recv()
        t = dhp[y, khalf, :].astype(F32) + dhc[y].astype(F32)
        for j in range(3):
            t = t + dhy[j].astype(F32)
        dht[...] = t

    def transpose_tokens():
        @pl.loop(0, DW // BLK)
        def _(i):
            cs = pl.ds(pl.multiple_of(i * BLK, BLK), BLK)
            xt[cs, :] = x_all[:, cs].astype(F32).T.astype(BF16)

    def weight_grads(first, last):
        @pl.loop(first, last)
        def _(j):
            acc = nn(xt[...], act[:, pl.ds(pl.multiple_of(j * 256, 256), 256)])
            cs = pl.ds(pl.multiple_of(j * BLK, BLK), BLK)
            for i in range(DW // BLK):
                f = flags[j, i].astype(F32)
                blk = acc[i * BLK:(i + 1) * BLK] * f
                ggate_ref[i * BLK:(i + 1) * BLK, cs] = blk[:, :BLK].astype(BF16)
                gup_ref[i * BLK:(i + 1) * BLK, cs] = blk[:, BLK:].astype(BF16)


    def down_grads(first, last):
        @pl.loop(first, last)
        def _(j):
            hidt[...] = hid[j].astype(F32).T.astype(BF16)
            acc = nn(hidt[...], dy[...])
            cs = pl.ds(pl.multiple_of(j * BLK, BLK), BLK)
            for i in range(DW // BLK):
                f = flags[j, i].astype(F32)
                gdown_ref[cs, i * BLK:(i + 1) * BLK] = (acc[:, i * BLK:(i + 1) * BLK] * f).astype(BF16)


    def pieces_perm():
        def column():
            ocol[...] = jnp.broadcast_to(order[...].reshape(1, TOK), (BLK, TOK)).astype(F32).T

        def block(q, p):
            lane = lax.broadcasted_iota(jnp.int32, (PLANE, BLK), 1).astype(F32)
            o = ocol[pl.ds(pl.multiple_of(zrel(RHO[q][p]) * PLANE, 32), PLANE), :]
            for j in range(TOK // BLK):
                perm[rows_of(q, p), j * BLK:(j + 1) * BLK] = jnp.where(o == lane + float(j * BLK), 1.0, 0.0).astype(BF16)

        return [column] + [functools.partial(block, q, p) for q in range(NQ) for p in range(2)]

    def pieces_transpose():
        def one(j):
            wgut[j * 256:(j + 1) * 256, :] = wgu[j].astype(F32).T.astype(BF16)

        return [functools.partial(one, j) for j in range(NY)]

    def make_perm():
        for piece in pieces_perm():
            piece()

    def pieces_masks():
        def wait():
            for cp in loads[2:]:
                cp.wait()

        return [wait] + [functools.partial(masks, i, i + 1) for i in range(DW // BLK)]

    T.start()
    G.start()
    T.step(1, pieces_masks()[:4])
    G.step(1, pieces_masks()[4:])
    T.step(2, pieces_perm()[:5])
    G.step(2, pieces_perm()[5:])
    T.step(3, pieces_transpose())
    G.step(3, pieces_p(0))
    T.step(4, pieces_g(0))
    stage_c(0)
    G.step(4, pieces_p(1))
    T.step(5, pieces_g(1))
    stage_c(1)
    G.step(5, pieces_p(2))
    gpair(2)
    gpair(3)
    dh_partial()
    stage_p(3)
    stage_c(2)
    dh_pair()
    stage_c(3)
    permute()
    transpose_tokens()
    dh_total()
    stage_y(2)
    stage_y(1)
    stage_a(2)
    stage_y(3)
    stage_a(1)
    stage_b(2)
    stage_y(0)
    stage_e()
    stage_a(3)
    stage_b(1)
    stage_a(0)
    stage_b(3)
    stage_x(2)
    stage_b(0)
    stage_x(1)
    stage_f()
    stage_x(3)
    weight_grads(0, 2)
    stage_k()
    down_grads(0, 1)
    stage_x(0)
    weight_grads(2, 4)
    down_grads(1, 4)
    for d in (1, 7, 2, 6, 3, 5, 4):
        rz_copy(d, zsrc.at[0, 0]).wait_recv()
    t = zsrc[0, 0].astype(F32)
    for j in range(NZ - 1):
        t = t + zrecv[j].astype(F32)
    gin_ref[...] = jnp.concatenate([t[:ROWS], t[ROWS:]], axis=1).astype(BF16)

    for cp in started:
        cp.wait_send()


def copy_kernel(a, b, c, d, oa, ob, oc, od, sem):
    stores = []
    for src, dst, n in ((b, ob, 4), (c, oc, 4), (d, od, 4), (a, oa, 1)):
        step = src.shape[0] // n
        for i in range(n):
            rows = pl.ds(i * step, step)
            stores.append(pltpu.make_async_copy(src.at[rows], dst.at[rows], sem.at[len(stores)]))
            stores[-1].start()
    for cp in stores:
        cp.wait()


def on_device(tokens, grad_out, w_gate, w_up, w_down, block_flags, token_order):
    vmem = pl.BlockSpec(memory_space=pltpu.VMEM)
    smem = pl.BlockSpec(memory_space=pltpu.SMEM)
    hbm = pl.BlockSpec(memory_space=pl.ANY)
    V = pltpu.VMEM
    n = NZ * NX
    half_slab = (n, 2 * ROWS, DW // 4)
    sems = [5]
    for _ in range(2):
        for m in (3, 8 * NP, 8, 24):
            sems += [m, m]
    for m in (NQ, 3 * NQ, 4, 3 * NQ, 4 * NQ, 3 * NQ, 7, 3, 4):
        sems += [m, m]
    scratch = [
        V((ROWS, DW), BF16), V((ROWS, DW), BF16),
        V((DW, FW), BF16), V((DW, FW), BF16), V((FW, DW), BF16),
        V((NY, DW, 2 * BLK), BF16), V((2 * FW, DW), BF16), V((FW, DW), BF16),
        V(half_slab, BF16), V(half_slab, BF16), V(half_slab, BF16), V(half_slab, BF16),
        V((TOK, DW), BF16), V((TOK, DW), BF16), V((TOK, DW), BF16),
        V((DW, TOK), BF16), V((TOK, TOK), BF16), V((TOK, BLK), F32),
        V((NQ, NY, 2 * PLANE, 2 * BLK), BF16), V((NQ, NY, PLANE, 2 * BLK), BF16),
        V((NQ, NY - 1, PLANE, 2 * BLK), BF16), V((NQ, NY - 1, PLANE, 2 * BLK), BF16),
        V((TOK, FW), BF16), V((NY, TOK, BLK), BF16), V((NY, HALF, BLK), BF16),
        V((NY - 1, HALF, BLK), BF16), V((NY - 1, HALF, BLK), BF16), V((HALF, BLK), F32),
        V((TOK, 2 * FW), BF16), V((NY, TOK, BLK), BF16), V((BLK, TOK), BF16),
        V((2, 2 * PLANE, DW), F32),
        V((NQ, NX, 2) + SLAB, BF16), V((NQ, NX - 1, 2) + SLAB, BF16),
        V((NQ, 2) + SLAB, BF16), V((NZ - 1,) + SLAB, BF16),
    ] + [pltpu.SemaphoreType.DMA((m,)) for m in sems]
    out_shape = (
        jax.ShapeDtypeStruct((ROWS, DW), BF16),
        jax.ShapeDtypeStruct((DW, FW), BF16),
        jax.ShapeDtypeStruct((DW, FW), BF16),
        jax.ShapeDtypeStruct((FW, DW), BF16),
    )
    out = pl.pallas_call(
        kernel,
        out_shape=tuple(pltpu.VMEM(o.shape, o.dtype) for o in out_shape),
        in_specs=[hbm, hbm, hbm, hbm, hbm, smem, vmem],
        out_specs=(vmem,) * 4,
        scratch_shapes=scratch,
        compiler_params=pltpu.CompilerParams(
            collective_id=0, has_side_effects=True, vmem_limit_bytes=57 * 2**20),
        name="layer_backward",
    )(tokens, grad_out, w_gate, w_up, w_down, block_flags.T, token_order)
    return pl.pallas_call(
        copy_kernel,
        out_shape=out_shape,
        in_specs=[vmem] * 4,
        out_specs=(hbm,) * 4,
        scratch_shapes=[pltpu.SemaphoreType.DMA((13,))],
        compiler_params=pltpu.CompilerParams(vmem_limit_bytes=16 * 2**20),
        name="hand_over",
    )(*out)


def solution(mesh):
    return jax.shard_map(
        on_device,
        mesh=mesh,
        in_specs=(
            P("col", "row"), P("col", "row"), P("row", "col"), P("row", "col"),
            P("col", "row"), P("row", "col"), P(),
        ),
        out_specs=(P("col", "row"), P("row", "col"), P("row", "col"), P("col", "row")),
        check_vma=False,
    )
```

```python
import functools

import jax
import jax.numpy as jnp
from jax import lax
from jax.experimental import pallas as pl
from jax.experimental.pallas import tpu as pltpu
from jax.sharding import PartitionSpec as P

MESH = pl.DeviceIdType.MESH
F32 = jnp.float32
BF16 = jnp.bfloat16

NY, NK, NZ, NX = 4, 2, 8, 4
ROWS = 24
TOK = 768
HALF = TOK // 2
DW = 1024
FW = 512
BLK = 128
SLAB = (2 * ROWS, DW // 2)
PLANE = NX * ROWS
RHO = ((0, -1), (1, -2), (2, -3), (3, 4))
NQ = len(RHO)
NP = 2
SW = NX // NP


def nt(a, b):
    return lax.dot_general(a, b, (((1,), (1,)), ((), ())), preferred_element_type=F32)


def nn(a, b):
    return lax.dot_general(a, b, (((1,), (0,)), ((), ())), preferred_element_type=F32)


def kernel(tok_hbm, go_hbm, wg_hbm, wu_hbm, wd_hbm, flags, order,
           gin_ref, ggate_ref, gup_ref, gdown_ref,
           tok_ref, go_ref,
           raw_g, raw_u, raw_d, wgu, wgut, wd, ga, gb, ta, tb, x_all, g_all, dy, xt, perm, ocol,
           part, crecv, ssend, yrecv, dhu, dhp, dhc, dhs, dhy, dht, act, hid, hidt, dxf, rsx, xrecv, zsrc, zrecv,
           wsem, gxa_s, gxa_r, gza_s, gza_r, gzb_s, gzb_r, gxb_s, gxb_r,
           txa_s, txa_r, tza_s, tza_r, tzb_s, tzb_r, txb_s, txb_r,
           c_s, c_r, y_s, y_r, h_s, h_r, a_s, a_r, b_s, b_r, rx_s, rx_r, rz_s, rz_r, e_s, e_r, f_s, f_r):
    r = lax.axis_index("row")
    c = lax.axis_index("col")
    y, k, z, x = r // 2, lax.rem(r, 2), c // 4, lax.rem(c, 4)

    def at(dy_=0, dk=0, dz=0, dx=0):
        return (lax.rem(y + dy_ + NY, NY) * 2 + lax.rem(k + dk, 2),
                lax.rem(z + dz + NZ, NZ) * 4 + lax.rem(x + dx + NX, NX))

    def zrel(d):
        return lax.rem(z + d + 2 * NZ, NZ)

    def yrel(d):
        return lax.rem(y + d + NY, NY)

    def xrel(d):
        return lax.rem(x + d + NX, NX)

    started = []

    def rc(src, dst, ss, rs, dev):
        return pltpu.make_async_remote_copy(src_ref=src, dst_ref=dst, send_sem=ss, recv_sem=rs,
                                            device_id=dev, device_id_type=MESH)

    def go(cp):
        cp.start()
        started.append(cp)


    peers = ([dict(dx=d) for d in range(1, NX)] + [dict(dz=d) for d in (1, 7, 2, 6, 3, 5, 4)]
             + [dict(dy_=d) for d in range(1, NY)] + [dict(dk=1)])
    bar = pltpu.get_barrier_semaphore()
    for p in peers:
        pl.semaphore_signal(bar, inc=1, device_id=at(**p), device_id_type=MESH)

    loads = [pltpu.make_async_copy(s, d, wsem.at[i])
             for i, (s, d) in enumerate(((go_hbm, go_ref), (tok_hbm, tok_ref),
                                         (wd_hbm, raw_d), (wg_hbm, raw_g), (wu_hbm, raw_u)))]
    for cp in loads:
        cp.start()
    QW = DW // 4

    def to_slabs(ref, a, b):
        v = ref[...].astype(F32)
        a[c] = jnp.concatenate([v[:, :QW], v[:, QW:2 * QW]], axis=0).astype(BF16)
        b[c] = jnp.concatenate([v[:, 2 * QW:3 * QW], v[:, 3 * QW:]], axis=0).astype(BF16)

    loads[0].wait()
    to_slabs(go_ref, ga, gb)
    loads[1].wait()
    to_slabs(tok_ref, ta, tb)
    pl.semaphore_wait(bar, len(peers))

    class Gather:
        def __init__(self, a, b, xa_s, xa_r, za_s, za_r, zb_s, zb_r, xb_s, xb_r):
            self.a, self.b = a, b
            self.xa, self.za, self.zb, self.xb = (xa_s, xa_r), (za_s, za_r), (zb_s, zb_r), (xb_s, xb_r)

        def xa_copy(self, d, src):
            ref = self.a.at[src]
            return rc(ref, ref, self.xa[0].at[d - 1], self.xa[1].at[d - 1], at(dx=d))

        def za_copy(self, direction, s, j, src_rel):
            i = ((0 if direction == 1 else 4) + s - 1) * NP + j
            ref = self.a.at[pl.ds(zrel(src_rel) * NX + j * SW, SW)]
            return rc(ref, ref, self.za[0].at[i], self.za[1].at[i], at(dz=direction))

        def zb_copy(self, direction, s, src_rel):
            i = (0 if direction == 1 else 4) + s - 1
            src = zrel(src_rel) * NX + x
            ref = self.b.at[src]
            if s == 4:
                ref = self.b.at[src, :, pl.ds(0 if direction == 1 else QW // 2, QW // 2)]
            return rc(ref, ref, self.zb[0].at[i], self.zb[1].at[i], at(dz=direction))

        def xb_copy(self, rel, d, src):
            i = (rel % NZ) * 3 + d - 1
            ref = self.b.at[src]
            return rc(ref, ref, self.xb[0].at[i], self.xb[1].at[i], at(dx=d))

        def xb_send(self, rel):
            for d in (2, 1, 3):
                go(self.xb_copy(rel, d, zrel(rel) * NX + x))

        def xb_wait(self, rel):
            for d in (1, 3, 2):
                self.xb_copy(rel, d, zrel(rel) * NX + xrel(-d)).wait_recv()

        def start(self):
            for d in (2, 1, 3):
                go(self.xa_copy(d, c))
            go(self.zb_copy(1, 1, 0))
            go(self.zb_copy(-1, 1, 0))
            self.xb_send(0)

        def step(self, t, fill=()):
            fill = list(fill)

            def work():
                if fill:
                    fill.pop(0)()

            if t <= 4:
                for direction in (1, -1):
                    self.zb_copy(direction, t, -direction * t).wait_recv()
                    if t < 4:
                        go(self.zb_copy(direction, t + 1, -direction * t))
                        self.xb_send(-direction * t)
                    work()
                if t == 4:
                    self.xb_send(4)
            if t == 1:
                for d in (1, 3, 2):
                    self.xa_copy(d, z * NX + xrel(-d)).wait_recv()
                for j in range(NP):
                    for direction in (1, -1):
                        go(self.za_copy(direction, 1, j, 0))
                while fill:
                    work()
                return
            s = t - 1
            for j in range(NP):
                for direction in (1, -1):
                    mine = (j < NP // 2) == (direction == 1)
                    if s < 4 or mine:
                        self.za_copy(direction, s, j, -direction * s).wait_recv()
                    if s < 3 or (s == 3 and mine):
                        go(self.za_copy(direction, s + 1, j, -direction * s))
                work()
            while fill:
                work()

    G = Gather(ga, gb, gxa_s, gxa_r, gza_s, gza_r, gzb_s, gzb_r, gxb_s, gxb_r)
    T = Gather(ta, tb, txa_s, txa_r, tza_s, tza_r, tzb_s, tzb_r, txb_s, txb_r)

    def masks(i0, i1):
        @pl.loop(i0, i1)
        def _(i):
            rows = pl.ds(pl.multiple_of(i * BLK, BLK), BLK)
            for j in range(FW // BLK):
                f = flags[j, i].astype(F32)
                cs = slice(j * BLK, (j + 1) * BLK)
                wgu[j, rows, :BLK] = (raw_g[rows, cs].astype(F32) * f).astype(BF16)
                wgu[j, rows, BLK:] = (raw_u[rows, cs].astype(F32) * f).astype(BF16)
                wd[cs, rows] = (raw_d[cs, rows].astype(F32) * f).astype(BF16)

    def unslab(a, b, c0, dst, row0):
        rows = pl.ds(row0, 2 * ROWS)
        for n, buf in enumerate((a, b)):
            v, w = buf[c0].astype(F32), buf[c0 + 1].astype(F32)
            dst[rows, 2 * n * QW:(2 * n + 1) * QW] = jnp.concatenate([v[:ROWS], w[:ROWS]], axis=0).astype(BF16)
            dst[rows, (2 * n + 1) * QW:(2 * n + 2) * QW] = jnp.concatenate([v[ROWS:], w[ROWS:]], axis=0).astype(BF16)

    def rows_of(q, p):
        return slice(p * HALF + q * PLANE, p * HALF + (q + 1) * PLANE)

    def krows(q):
        return pl.ds(pl.multiple_of(k * HALF + q * PLANE, 32), PLANE)

    kplane = pl.ds(pl.multiple_of(k * PLANE, 32), PLANE)
    khalf = pl.ds(pl.multiple_of(k * HALF, HALF), HALF)

    def c_copy(q):
        sib = pl.ds(pl.multiple_of((1 - k) * PLANE, 32), PLANE)
        return rc(part.at[q, :, sib], crecv.at[q], c_s.at[q], c_r.at[q], at(dk=1))

    def pieces_p(q):
        def rows(p):
            plane = zrel(RHO[q][p])
            T.xb_wait(RHO[q][p])
            for xx in (0, 2):
                unslab(ta, tb, plane * NX + xx, x_all, p * HALF + q * PLANE + xx * ROWS)

        def product(d):
            lhs = jnp.concatenate([x_all[rows_of(q, 0), :], x_all[rows_of(q, 1), :]], axis=0)
            part[q, d] = nn(lhs, wgu[yrel(d)]).astype(BF16)
            if d == NY - 1:
                go(c_copy(q))

        return ([functools.partial(rows, p) for p in range(2)]
                + [functools.partial(product, d) for d in range(NY)])

    def stage_p(q):
        for piece in pieces_p(q):
            piece()

    def y_copy(q, d):
        i = q * 3 + d - 1
        return rc(ssend.at[q, d - 1], yrecv.at[q, d - 1], y_s.at[i], y_r.at[i], at(dy_=d))

    def stage_c(q):
        c_copy(q).wait_recv()
        for d in (2, 1, 3):
            ssend[q, d - 1] = (part[q, d, kplane, :].astype(F32) + crecv[q, d].astype(F32)).astype(BF16)
            go(y_copy(q, d))

    def a_copy(q, d, src):
        i = q * 3 + d - 1
        ref = act.at[krows(q), pl.ds(pl.multiple_of(src * 256, 256), 256)]
        return rc(ref, ref, a_s.at[i], a_r.at[i], at(dy_=d))

    def b_copy(q, d, src, half):
        i = q * 4 + d
        ref = act.at[pl.ds(pl.multiple_of(half * HALF + q * PLANE, 32), PLANE), pl.ds(pl.multiple_of(src * 256, 256), 256)]
        return rc(ref, ref, b_s.at[i], b_r.at[i], at(dk=1))

    def stage_y(q):
        for d in (1, 3, 2):
            y_copy(q, d).wait_recv()
        t = part[q, 0, kplane, :].astype(F32) + crecv[q, 0].astype(F32)
        for j in range(3):
            t = t + yrecv[q, j].astype(F32)
        gate, up = t[:, :BLK], t[:, BLK:]
        dh = dht[q * PLANE:(q + 1) * PLANE, :]
        sig = 1.0 / (1.0 + jnp.exp(-gate))
        silu = gate * sig
        rows = krows(q)
        act[rows, pl.ds(pl.multiple_of(y * 256, 256), BLK)] = (dh * up * sig * (1.0 + gate * (1.0 - sig))).astype(BF16)
        act[rows, pl.ds(pl.multiple_of(y * 256 + BLK, BLK), BLK)] = (dh * silu).astype(BF16)
        hid[y, rows, :] = (silu * up).astype(BF16)
        for d in (2, 1, 3):
            go(a_copy(q, d, y))
        go(b_copy(q, 0, y, k))

    def e_copy(d, src):
        ref = hid.at[src, khalf]
        return rc(ref, ref, e_s.at[d - 1], e_r.at[d - 1], at(dy_=d))

    def f_copy(d, half):
        ref = hid.at[yrel(-d), pl.ds(pl.multiple_of(half * HALF, HALF), HALF)]
        return rc(ref, ref, f_s.at[d], f_r.at[d], at(dk=1))

    def stage_e():
        for d in (2, 1, 3):
            go(e_copy(d, y))
        go(f_copy(0, k))

    def stage_f():
        for d in (1, 3, 2):
            e_copy(d, yrel(-d)).wait_recv()
            go(f_copy(d, k))

    def stage_k():
        for d in (0, 1, 3, 2):
            f_copy(d, 1 - k).wait_recv()

    def stage_a(q):
        for d in (1, 3, 2):
            a_copy(q, d, yrel(-d)).wait_recv()
            go(b_copy(q, d, yrel(-d), k))

    def rx_copy(q, p, d):
        i = (2 * q + p) * 3 + d - 1
        return rc(rsx.at[q, xrel(d), p], xrecv.at[q, d - 1, p], rx_s.at[i], rx_r.at[i], at(dx=d))

    def stage_b(q):
        for d in (0, 1, 3, 2):
            b_copy(q, d, yrel(-d), 1 - k).wait_recv()

        lhs = jnp.concatenate([act[rows_of(q, 0), :], act[rows_of(q, 1), :]], axis=0)

        @pl.loop(0, DW // 256)
        def _(i):
            cs = pl.ds(pl.multiple_of(i * 256, 256), 256)
            dxf[q % 2, :, cs] = nn(lhs, wgut[:, cs])

        for p in (1, 0):
            for xx in range(NX):
                v = dxf[q % 2, p * PLANE + xx * ROWS:p * PLANE + (xx + 1) * ROWS, :]
                rsx[q, xx, p] = jnp.concatenate([v[:, :DW // 2], v[:, DW // 2:]], axis=0).astype(BF16)
            for d in (2, 1, 3):
                go(rx_copy(q, p, d))

    def rz_copy(rho, src):
        i = rho % NZ - 1
        return rc(src, zrecv.at[i], rz_s.at[i], rz_r.at[i], at(dz=rho))

    def stage_x(q):
        for p in (1, 0):
            for d in (1, 3, 2):
                rx_copy(q, p, d).wait_recv()
            t = rsx[q, x, p].astype(F32)
            for j in range(3):
                t = t + xrecv[q, j, p].astype(F32)
            zsrc[q, p] = t.astype(BF16)
            if RHO[q][p] != 0:
                go(rz_copy(RHO[q][p], zsrc.at[q, p]))

    def h_copy(d):
        if d == 0:
            sib = pl.ds(pl.multiple_of((1 - k) * HALF, HALF), HALF)
            return rc(dhp.at[:, sib], dhc, h_s.at[0], h_r.at[0], at(dk=1))
        return rc(dhs.at[d - 1], dhy.at[d - 1], h_s.at[d], h_r.at[d], at(dy_=d))

    def pieces_g(q):
        parts = [pl.ds(pl.multiple_of(zrel(RHO[q][p]) * PLANE, 32), PLANE) for p in range(2)]

        def rows(p):
            plane = zrel(RHO[q][p])
            G.xb_wait(RHO[q][p])
            for xx in (0, 2):
                unslab(ga, gb, plane * NX + xx, g_all, pl.multiple_of(plane * PLANE + xx * ROWS, 2 * ROWS))

        def product(i):
            lhs = jnp.concatenate([g_all[parts[0], :], g_all[parts[1], :]], axis=0)
            t = nt(lhs, wd[i * 256:(i + 1) * 256, :]).astype(BF16)
            dhu[parts[0], i * 256:(i + 1) * 256] = t[:PLANE]
            dhu[parts[1], i * 256:(i + 1) * 256] = t[PLANE:]

        return ([functools.partial(rows, p) for p in range(2)]
                + [functools.partial(product, i) for i in range(2)])

    def gpair(q):
        for piece in pieces_g(q):
            piece()

    def permute():
        @pl.loop(0, DW // 256)
        def _(i):
            cs = pl.ds(pl.multiple_of(i * 256, 256), 256)
            dy[:, cs] = nn(perm[...], g_all[:, cs]).astype(BF16)

    def dh_partial():
        for i in range(2):
            t = nn(perm[...], dhu[:, i * 256:(i + 1) * 256])
            dhp[2 * i] = t[:, :BLK].astype(BF16)
            dhp[2 * i + 1] = t[:, BLK:].astype(BF16)
        go(h_copy(0))

    def dh_pair():
        h_copy(0).wait_recv()
        for d in (2, 1, 3):
            yb = yrel(d)
            dhs[d - 1] = (dhp[yb, khalf, :].astype(F32) + dhc[yb].astype(F32)).astype(BF16)
            go(h_copy(d))

    def dh_total():
        for d in (1, 3, 2):
            h_copy(d).wait_recv()
        t = dhp[y, khalf, :].astype(F32) + dhc[y].astype(F32)
        for j in range(3):
            t = t + dhy[j].astype(F32)
        dht[...] = t

    def transpose_tokens():
        @pl.loop(0, DW // BLK)
        def _(i):
            cs = pl.ds(pl.multiple_of(i * BLK, BLK), BLK)
            xt[cs, :] = x_all[:, cs].astype(F32).T.astype(BF16)

    def weight_grads(first, last):
        @pl.loop(first, last)
        def _(j):
            acc = nn(xt[...], act[:, pl.ds(pl.multiple_of(j * 256, 256), 256)])
            cs = pl.ds(pl.multiple_of(j * BLK, BLK), BLK)
            for i in range(DW // BLK):
                f = flags[j, i].astype(F32)
                blk = acc[i * BLK:(i + 1) * BLK] * f
                ggate_ref[i * BLK:(i + 1) * BLK, cs] = blk[:, :BLK].astype(BF16)
                gup_ref[i * BLK:(i + 1) * BLK, cs] = blk[:, BLK:].astype(BF16)


    def down_grads(first, last):
        @pl.loop(first, last)
        def _(j):
            hidt[...] = hid[j].astype(F32).T.astype(BF16)
            acc = nn(hidt[...], dy[...])
            cs = pl.ds(pl.multiple_of(j * BLK, BLK), BLK)
            for i in range(DW // BLK):
                f = flags[j, i].astype(F32)
                gdown_ref[cs, i * BLK:(i + 1) * BLK] = (acc[:, i * BLK:(i + 1) * BLK] * f).astype(BF16)


    def pieces_perm():
        def column():
            ocol[...] = jnp.broadcast_to(order[...].reshape(1, TOK), (BLK, TOK)).astype(F32).T

        def block(q, p):
            lane = lax.broadcasted_iota(jnp.int32, (PLANE, BLK), 1).astype(F32)
            o = ocol[pl.ds(pl.multiple_of(zrel(RHO[q][p]) * PLANE, 32), PLANE), :]
            for j in range(TOK // BLK):
                perm[rows_of(q, p), j * BLK:(j + 1) * BLK] = jnp.where(o == lane + float(j * BLK), 1.0, 0.0).astype(BF16)

        return [column] + [functools.partial(block, q, p) for q in range(NQ) for p in range(2)]

    def pieces_transpose():
        def one(j):
            wgut[j * 256:(j + 1) * 256, :] = wgu[j].astype(F32).T.astype(BF16)

        return [functools.partial(one, j) for j in range(NY)]

    def make_perm():
        for piece in pieces_perm():
            piece()

    def pieces_masks():
        def wait():
            for cp in loads[2:]:
                cp.wait()

        return [wait] + [functools.partial(masks, i, i + 1) for i in range(DW // BLK)]

    T.start()
    G.start()
    T.step(1, pieces_masks()[:4])
    G.step(1, pieces_masks()[4:])
    T.step(2, pieces_perm()[:5])
    G.step(2, pieces_perm()[5:])
    T.step(3, pieces_transpose())
    G.step(3, pieces_p(0))
    T.step(4, pieces_g(0))
    stage_c(0)
    G.step(4, pieces_p(1))
    T.step(5, pieces_g(1))
    stage_c(1)
    G.step(5, pieces_p(2))
    gpair(2)
    gpair(3)
    dh_partial()
    stage_p(3)
    stage_c(2)
    dh_pair()
    stage_c(3)
    permute()
    transpose_tokens()
    dh_total()
    stage_y(2)
    stage_y(1)
    stage_a(2)
    stage_y(3)
    stage_a(1)
    stage_b(2)
    stage_y(0)
    stage_e()
    stage_a(3)
    stage_b(1)
    stage_a(0)
    stage_b(3)
    stage_x(2)
    stage_b(0)
    stage_x(1)
    stage_f()
    weight_grads(0, 2)
    stage_x(3)
    stage_k()
    down_grads(0, 1)
    stage_x(0)
    weight_grads(2, 4)
    down_grads(1, 4)
    for d in (1, 7, 2, 6, 3, 5, 4):
        rz_copy(d, zsrc.at[0, 0]).wait_recv()
    t = zsrc[0, 0].astype(F32)
    for j in range(NZ - 1):
        t = t + zrecv[j].astype(F32)
    gin_ref[...] = jnp.concatenate([t[:ROWS], t[ROWS:]], axis=1).astype(BF16)

    for cp in started:
        cp.wait_send()


def copy_kernel(a, b, c, d, oa, ob, oc, od, sem):
    stores = []
    for src, dst, n in ((b, ob, 4), (c, oc, 4), (d, od, 4), (a, oa, 1)):
        step = src.shape[0] // n
        for i in range(n):
            rows = pl.ds(i * step, step)
            stores.append(pltpu.make_async_copy(src.at[rows], dst.at[rows], sem.at[len(stores)]))
            stores[-1].start()
    for cp in stores:
        cp.wait()


def on_device(tokens, grad_out, w_gate, w_up, w_down, block_flags, token_order):
    vmem = pl.BlockSpec(memory_space=pltpu.VMEM)
    smem = pl.BlockSpec(memory_space=pltpu.SMEM)
    hbm = pl.BlockSpec(memory_space=pl.ANY)
    V = pltpu.VMEM
    n = NZ * NX
    half_slab = (n, 2 * ROWS, DW // 4)
    sems = [5]
    for _ in range(2):
        for m in (3, 8 * NP, 8, 24):
            sems += [m, m]
    for m in (NQ, 3 * NQ, 4, 3 * NQ, 4 * NQ, 6 * NQ, 7, 3, 4):
        sems += [m, m]
    scratch = [
        V((ROWS, DW), BF16), V((ROWS, DW), BF16),
        V((DW, FW), BF16), V((DW, FW), BF16), V((FW, DW), BF16),
        V((NY, DW, 2 * BLK), BF16), V((2 * FW, DW), BF16), V((FW, DW), BF16),
        V(half_slab, BF16), V(half_slab, BF16), V(half_slab, BF16), V(half_slab, BF16),
        V((TOK, DW), BF16), V((TOK, DW), BF16), V((TOK, DW), BF16),
        V((DW, TOK), BF16), V((TOK, TOK), BF16), V((TOK, BLK), F32),
        V((NQ, NY, 2 * PLANE, 2 * BLK), BF16), V((NQ, NY, PLANE, 2 * BLK), BF16),
        V((NQ, NY - 1, PLANE, 2 * BLK), BF16), V((NQ, NY - 1, PLANE, 2 * BLK), BF16),
        V((TOK, FW), BF16), V((NY, TOK, BLK), BF16), V((NY, HALF, BLK), BF16),
        V((NY - 1, HALF, BLK), BF16), V((NY - 1, HALF, BLK), BF16), V((HALF, BLK), F32),
        V((TOK, 2 * FW), BF16), V((NY, TOK, BLK), BF16), V((BLK, TOK), BF16),
        V((2, 2 * PLANE, DW), F32),
        V((NQ, NX, 2) + SLAB, BF16), V((NQ, NX - 1, 2) + SLAB, BF16),
        V((NQ, 2) + SLAB, BF16), V((NZ - 1,) + SLAB, BF16),
    ] + [pltpu.SemaphoreType.DMA((m,)) for m in sems]
    out_shape = (
        jax.ShapeDtypeStruct((ROWS, DW), BF16),
        jax.ShapeDtypeStruct((DW, FW), BF16),
        jax.ShapeDtypeStruct((DW, FW), BF16),
        jax.ShapeDtypeStruct((FW, DW), BF16),
    )
    out = pl.pallas_call(
        kernel,
        out_shape=tuple(pltpu.VMEM(o.shape, o.dtype) for o in out_shape),
        in_specs=[hbm, hbm, hbm, hbm, hbm, smem, vmem],
        out_specs=(vmem,) * 4,
        scratch_shapes=scratch,
        compiler_params=pltpu.CompilerParams(
            collective_id=0, has_side_effects=True, vmem_limit_bytes=57 * 2**20),
        name="layer_backward",
    )(tokens, grad_out, w_gate, w_up, w_down, block_flags.T, token_order)
    return pl.pallas_call(
        copy_kernel,
        out_shape=out_shape,
        in_specs=[vmem] * 4,
        out_specs=(hbm,) * 4,
        scratch_shapes=[pltpu.SemaphoreType.DMA((13,))],
        compiler_params=pltpu.CompilerParams(vmem_limit_bytes=16 * 2**20),
        name="hand_over",
    )(*out)


def solution(mesh):
    return jax.shard_map(
        on_device,
        mesh=mesh,
        in_specs=(
            P("col", "row"), P("col", "row"), P("row", "col"), P("row", "col"),
            P("col", "row"), P("row", "col"), P(),
        ),
        out_specs=(P("col", "row"), P("row", "col"), P("row", "col"), P("col", "row")),
        check_vma=False,
    )
```

```python
import functools

import jax
import jax.numpy as jnp
from jax import lax
from jax.experimental import pallas as pl
from jax.experimental.pallas import tpu as pltpu
from jax.sharding import PartitionSpec as P

MESH = pl.DeviceIdType.MESH
F32 = jnp.float32
BF16 = jnp.bfloat16

NY, NK, NZ, NX = 4, 2, 8, 4
ROWS = 24
TOK = 768
HALF = TOK // 2
DW = 1024
FW = 512
BLK = 128
SLAB = (2 * ROWS, DW // 2)
PLANE = NX * ROWS
RHO = ((0, -1), (1, -2), (2, -3), (3, 4))
NQ = len(RHO)
NP = 2
SW = NX // NP


def nt(a, b):
    return lax.dot_general(a, b, (((1,), (1,)), ((), ())), preferred_element_type=F32)


def nn(a, b):
    return lax.dot_general(a, b, (((1,), (0,)), ((), ())), preferred_element_type=F32)


def kernel(tok_hbm, go_hbm, wg_hbm, wu_hbm, wd_hbm, flags, order,
           gin_ref, ggate_ref, gup_ref, gdown_ref,
           tok_ref, go_ref,
           raw_g, raw_u, raw_d, wgu, wgut, wd, ga, gb, ta, tb, x_all, g_all, dy, xt, perm, ocol,
           part, crecv, ssend, yrecv, dhu, dhp, dhc, dhs, dhy, dht, act, hid, hidt, dxf, rsx, xrecv, zsrc, zrecv,
           wsem, gxa_s, gxa_r, gza_s, gza_r, gzb_s, gzb_r, gxb_s, gxb_r,
           txa_s, txa_r, tza_s, tza_r, tzb_s, tzb_r, txb_s, txb_r,
           c_s, c_r, y_s, y_r, h_s, h_r, a_s, a_r, b_s, b_r, rx_s, rx_r, rz_s, rz_r, e_s, e_r, f_s, f_r):
    r = lax.axis_index("row")
    c = lax.axis_index("col")
    y, k, z, x = r // 2, lax.rem(r, 2), c // 4, lax.rem(c, 4)

    def at(dy_=0, dk=0, dz=0, dx=0):
        return (lax.rem(y + dy_ + NY, NY) * 2 + lax.rem(k + dk, 2),
                lax.rem(z + dz + NZ, NZ) * 4 + lax.rem(x + dx + NX, NX))

    def zrel(d):
        return lax.rem(z + d + 2 * NZ, NZ)

    def yrel(d):
        return lax.rem(y + d + NY, NY)

    def xrel(d):
        return lax.rem(x + d + NX, NX)

    started = []

    def rc(src, dst, ss, rs, dev):
        return pltpu.make_async_remote_copy(src_ref=src, dst_ref=dst, send_sem=ss, recv_sem=rs,
                                            device_id=dev, device_id_type=MESH)

    def go(cp):
        cp.start()
        started.append(cp)


    peers = ([dict(dx=d) for d in range(1, NX)] + [dict(dz=d) for d in (1, 7, 2, 6, 3, 5, 4)]
             + [dict(dy_=d) for d in range(1, NY)] + [dict(dk=1)])
    bar = pltpu.get_barrier_semaphore()
    for p in peers:
        pl.semaphore_signal(bar, inc=1, device_id=at(**p), device_id_type=MESH)

    loads = [pltpu.make_async_copy(s, d, wsem.at[i])
             for i, (s, d) in enumerate(((go_hbm, go_ref), (tok_hbm, tok_ref),
                                         (wd_hbm, raw_d), (wg_hbm, raw_g), (wu_hbm, raw_u)))]
    for cp in loads:
        cp.start()
    QW = DW // 4

    def to_slabs(ref, a, b):
        v = ref[...].astype(F32)
        a[c] = jnp.concatenate([v[:, :QW], v[:, QW:2 * QW]], axis=0).astype(BF16)
        b[c] = jnp.concatenate([v[:, 2 * QW:3 * QW], v[:, 3 * QW:]], axis=0).astype(BF16)

    loads[0].wait()
    to_slabs(go_ref, ga, gb)
    loads[1].wait()
    to_slabs(tok_ref, ta, tb)
    pl.semaphore_wait(bar, len(peers))

    class Gather:
        def __init__(self, a, b, xa_s, xa_r, za_s, za_r, zb_s, zb_r, xb_s, xb_r):
            self.a, self.b = a, b
            self.xa, self.za, self.zb, self.xb = (xa_s, xa_r), (za_s, za_r), (zb_s, zb_r), (xb_s, xb_r)

        def xa_copy(self, d, src):
            ref = self.a.at[src]
            return rc(ref, ref, self.xa[0].at[d - 1], self.xa[1].at[d - 1], at(dx=d))

        def za_copy(self, direction, s, j, src_rel):
            i = ((0 if direction == 1 else 4) + s - 1) * NP + j
            ref = self.a.at[pl.ds(zrel(src_rel) * NX + j * SW, SW)]
            return rc(ref, ref, self.za[0].at[i], self.za[1].at[i], at(dz=direction))

        def zb_copy(self, direction, s, src_rel):
            i = (0 if direction == 1 else 4) + s - 1
            src = zrel(src_rel) * NX + x
            ref = self.b.at[src]
            if s == 4:
                ref = self.b.at[src, :, pl.ds(0 if direction == 1 else QW // 2, QW // 2)]
            return rc(ref, ref, self.zb[0].at[i], self.zb[1].at[i], at(dz=direction))

        def xb_copy(self, rel, d, src):
            i = (rel % NZ) * 3 + d - 1
            ref = self.b.at[src]
            return rc(ref, ref, self.xb[0].at[i], self.xb[1].at[i], at(dx=d))

        def xb_send(self, rel):
            for d in (1, 3, 2):
                go(self.xb_copy(rel, d, zrel(rel) * NX + x))

        def xb_wait(self, rel):
            for d in (1, 3, 2):
                self.xb_copy(rel, d, zrel(rel) * NX + xrel(-d)).wait_recv()

        def start(self):
            for d in (1, 3, 2):
                go(self.xa_copy(d, c))
            go(self.zb_copy(1, 1, 0))
            go(self.zb_copy(-1, 1, 0))
            self.xb_send(0)

        def step(self, t, fill=()):
            fill = list(fill)

            def work():
                if fill:
                    fill.pop(0)()

            if t <= 4:
                for direction in (1, -1):
                    self.zb_copy(direction, t, -direction * t).wait_recv()
                    if t < 4:
                        go(self.zb_copy(direction, t + 1, -direction * t))
                        self.xb_send(-direction * t)
                    work()
                if t == 4:
                    self.xb_send(4)
            if t == 1:
                for d in (1, 3, 2):
                    self.xa_copy(d, z * NX + xrel(-d)).wait_recv()
                for j in range(NP):
                    for direction in (1, -1):
                        go(self.za_copy(direction, 1, j, 0))
                while fill:
                    work()
                return
            s = t - 1
            for j in range(NP):
                for direction in (1, -1):
                    mine = (j < NP // 2) == (direction == 1)
                    if s < 4 or mine:
                        self.za_copy(direction, s, j, -direction * s).wait_recv()
                    if s < 3 or (s == 3 and mine):
                        go(self.za_copy(direction, s + 1, j, -direction * s))
                work()
            while fill:
                work()

    G = Gather(ga, gb, gxa_s, gxa_r, gza_s, gza_r, gzb_s, gzb_r, gxb_s, gxb_r)
    T = Gather(ta, tb, txa_s, txa_r, tza_s, tza_r, tzb_s, tzb_r, txb_s, txb_r)

    def masks(i0, i1):
        @pl.loop(i0, i1)
        def _(i):
            rows = pl.ds(pl.multiple_of(i * BLK, BLK), BLK)
            for j in range(FW // BLK):
                f = flags[j, i].astype(F32)
                cs = slice(j * BLK, (j + 1) * BLK)
                wgu[j, rows, :BLK] = (raw_g[rows, cs].astype(F32) * f).astype(BF16)
                wgu[j, rows, BLK:] = (raw_u[rows, cs].astype(F32) * f).astype(BF16)
                wd[cs, rows] = (raw_d[cs, rows].astype(F32) * f).astype(BF16)

    def unslab(a, b, c0, dst, row0):
        rows = pl.ds(row0, 2 * ROWS)
        for n, buf in enumerate((a, b)):
            v, w = buf[c0].astype(F32), buf[c0 + 1].astype(F32)
            dst[rows, 2 * n * QW:(2 * n + 1) * QW] = jnp.concatenate([v[:ROWS], w[:ROWS]], axis=0).astype(BF16)
            dst[rows, (2 * n + 1) * QW:(2 * n + 2) * QW] = jnp.concatenate([v[ROWS:], w[ROWS:]], axis=0).astype(BF16)

    def rows_of(q, p):
        return slice(p * HALF + q * PLANE, p * HALF + (q + 1) * PLANE)

    def krows(q):
        return pl.ds(pl.multiple_of(k * HALF + q * PLANE, 32), PLANE)

    kplane = pl.ds(pl.multiple_of(k * PLANE, 32), PLANE)
    khalf = pl.ds(pl.multiple_of(k * HALF, HALF), HALF)

    def c_copy(q):
        sib = pl.ds(pl.multiple_of((1 - k) * PLANE, 32), PLANE)
        return rc(part.at[q, :, sib], crecv.at[q], c_s.at[q], c_r.at[q], at(dk=1))

    def pieces_p(q):
        def rows(p):
            plane = zrel(RHO[q][p])
            T.xb_wait(RHO[q][p])
            for xx in (0, 2):
                unslab(ta, tb, plane * NX + xx, x_all, p * HALF + q * PLANE + xx * ROWS)

        def product(d):
            lhs = jnp.concatenate([x_all[rows_of(q, 0), :], x_all[rows_of(q, 1), :]], axis=0)
            part[q, d] = nn(lhs, wgu[yrel(d)]).astype(BF16)
            if d == NY - 1:
                go(c_copy(q))

        return ([functools.partial(rows, p) for p in range(2)]
                + [functools.partial(product, d) for d in range(NY)])

    def stage_p(q):
        for piece in pieces_p(q):
            piece()

    def y_copy(q, d):
        i = q * 3 + d - 1
        return rc(ssend.at[q, d - 1], yrecv.at[q, d - 1], y_s.at[i], y_r.at[i], at(dy_=d))

    def stage_c(q):
        c_copy(q).wait_recv()
        for d in (1, 3, 2):
            ssend[q, d - 1] = (part[q, d, kplane, :].astype(F32) + crecv[q, d].astype(F32)).astype(BF16)
            go(y_copy(q, d))

    def a_copy(q, d, src):
        i = q * 3 + d - 1
        ref = act.at[krows(q), pl.ds(pl.multiple_of(src * 256, 256), 256)]
        return rc(ref, ref, a_s.at[i], a_r.at[i], at(dy_=d))

    def b_copy(q, d, src, half):
        i = q * 4 + d
        ref = act.at[pl.ds(pl.multiple_of(half * HALF + q * PLANE, 32), PLANE), pl.ds(pl.multiple_of(src * 256, 256), 256)]
        return rc(ref, ref, b_s.at[i], b_r.at[i], at(dk=1))

    def stage_y(q):
        for d in (1, 3, 2):
            y_copy(q, d).wait_recv()
        t = part[q, 0, kplane, :].astype(F32) + crecv[q, 0].astype(F32)
        for j in range(3):
            t = t + yrecv[q, j].astype(F32)
        gate, up = t[:, :BLK], t[:, BLK:]
        dh = dht[q * PLANE:(q + 1) * PLANE, :]
        sig = 1.0 / (1.0 + jnp.exp(-gate))
        silu = gate * sig
        rows = krows(q)
        act[rows, pl.ds(pl.multiple_of(y * 256, 256), BLK)] = (dh * up * sig * (1.0 + gate * (1.0 - sig))).astype(BF16)
        act[rows, pl.ds(pl.multiple_of(y * 256 + BLK, BLK), BLK)] = (dh * silu).astype(BF16)
        hid[y, rows, :] = (silu * up).astype(BF16)
        for d in (1, 3, 2):
            go(a_copy(q, d, y))
        go(b_copy(q, 0, y, k))

    def e_copy(d, src):
        ref = hid.at[src, khalf]
        return rc(ref, ref, e_s.at[d - 1], e_r.at[d - 1], at(dy_=d))

    def f_copy(d, half):
        ref = hid.at[yrel(-d), pl.ds(pl.multiple_of(half * HALF, HALF), HALF)]
        return rc(ref, ref, f_s.at[d], f_r.at[d], at(dk=1))

    def stage_e():
        for d in (1, 3, 2):
            go(e_copy(d, y))
        go(f_copy(0, k))

    def stage_f():
        for d in (1, 3, 2):
            e_copy(d, yrel(-d)).wait_recv()
            go(f_copy(d, k))

    def stage_k():
        for d in (0, 1, 3, 2):
            f_copy(d, 1 - k).wait_recv()

    def stage_a(q):
        for d in (1, 3, 2):
            a_copy(q, d, yrel(-d)).wait_recv()
            go(b_copy(q, d, yrel(-d), k))

    def rx_copy(q, p, d):
        i = (2 * q + p) * 3 + d - 1
        return rc(rsx.at[q, xrel(d), p], xrecv.at[q, d - 1, p], rx_s.at[i], rx_r.at[i], at(dx=d))

    def stage_b(q):
        for d in (0, 1, 3, 2):
            b_copy(q, d, yrel(-d), 1 - k).wait_recv()

        lhs = jnp.concatenate([act[rows_of(q, 0), :], act[rows_of(q, 1), :]], axis=0)

        @pl.loop(0, DW // 256)
        def _(i):
            cs = pl.ds(pl.multiple_of(i * 256, 256), 256)
            dxf[q % 2, :, cs] = nn(lhs, wgut[:, cs])

        for p in (1, 0):
            for xx in range(NX):
                v = dxf[q % 2, p * PLANE + xx * ROWS:p * PLANE + (xx + 1) * ROWS, :]
                rsx[q, xx, p] = jnp.concatenate([v[:, :DW // 2], v[:, DW // 2:]], axis=0).astype(BF16)
            for d in (1, 3, 2):
                go(rx_copy(q, p, d))

    def rz_copy(rho, src):
        i = rho % NZ - 1
        return rc(src, zrecv.at[i], rz_s.at[i], rz_r.at[i], at(dz=rho))

    def stage_x(q):
        for p in (1, 0):
            for d in (1, 3, 2):
                rx_copy(q, p, d).wait_recv()
            t = rsx[q, x, p].astype(F32)
            for j in range(3):
                t = t + xrecv[q, j, p].astype(F32)
            zsrc[q, p] = t.astype(BF16)
            if RHO[q][p] != 0:
                go(rz_copy(RHO[q][p], zsrc.at[q, p]))

    def h_copy(d):
        if d == 0:
            sib = pl.ds(pl.multiple_of((1 - k) * HALF, HALF), HALF)
            return rc(dhp.at[:, sib], dhc, h_s.at[0], h_r.at[0], at(dk=1))
        return rc(dhs.at[d - 1], dhy.at[d - 1], h_s.at[d], h_r.at[d], at(dy_=d))

    def pieces_g(q):
        parts = [pl.ds(pl.multiple_of(zrel(RHO[q][p]) * PLANE, 32), PLANE) for p in range(2)]

        def rows(p):
            plane = zrel(RHO[q][p])
            G.xb_wait(RHO[q][p])
            for xx in (0, 2):
                unslab(ga, gb, plane * NX + xx, g_all, pl.multiple_of(plane * PLANE + xx * ROWS, 2 * ROWS))

        def product(i):
            lhs = jnp.concatenate([g_all[parts[0], :], g_all[parts[1], :]], axis=0)
            t = nt(lhs, wd[i * 256:(i + 1) * 256, :]).astype(BF16)
            dhu[parts[0], i * 256:(i + 1) * 256] = t[:PLANE]
            dhu[parts[1], i * 256:(i + 1) * 256] = t[PLANE:]

        return ([functools.partial(rows, p) for p in range(2)]
                + [functools.partial(product, i) for i in range(2)])

    def gpair(q):
        for piece in pieces_g(q):
            piece()

    def permute():
        @pl.loop(0, DW // 256)
        def _(i):
            cs = pl.ds(pl.multiple_of(i * 256, 256), 256)
            dy[:, cs] = nn(perm[...], g_all[:, cs]).astype(BF16)

    def dh_partial():
        for i in range(2):
            t = nn(perm[...], dhu[:, i * 256:(i + 1) * 256])
            dhp[2 * i] = t[:, :BLK].astype(BF16)
            dhp[2 * i + 1] = t[:, BLK:].astype(BF16)
        go(h_copy(0))

    def dh_pair():
        h_copy(0).wait_recv()
        for d in (1, 3, 2):
            yb = yrel(d)
            dhs[d - 1] = (dhp[yb, khalf, :].astype(F32) + dhc[yb].astype(F32)).astype(BF16)
            go(h_copy(d))

    def dh_total():
        for d in (1, 3, 2):
            h_copy(d).wait_recv()
        t = dhp[y, khalf, :].astype(F32) + dhc[y].astype(F32)
        for j in range(3):
            t = t + dhy[j].astype(F32)
        dht[...] = t

    def transpose_tokens():
        @pl.loop(0, DW // BLK)
        def _(i):
            cs = pl.ds(pl.multiple_of(i * BLK, BLK), BLK)
            xt[cs, :] = x_all[:, cs].astype(F32).T.astype(BF16)

    def weight_grads(first, last):
        @pl.loop(first, last)
        def _(j):
            acc = nn(xt[...], act[:, pl.ds(pl.multiple_of(j * 256, 256), 256)])
            cs = pl.ds(pl.multiple_of(j * BLK, BLK), BLK)
            for i in range(DW // BLK):
                f = flags[j, i].astype(F32)
                blk = acc[i * BLK:(i + 1) * BLK] * f
                ggate_ref[i * BLK:(i + 1) * BLK, cs] = blk[:, :BLK].astype(BF16)
                gup_ref[i * BLK:(i + 1) * BLK, cs] = blk[:, BLK:].astype(BF16)


    def down_grads(first, last):
        @pl.loop(first, last)
        def _(j):
            hidt[...] = hid[j].astype(F32).T.astype(BF16)
            acc = nn(hidt[...], dy[...])
            cs = pl.ds(pl.multiple_of(j * BLK, BLK), BLK)
            for i in range(DW // BLK):
                f = flags[j, i].astype(F32)
                gdown_ref[cs, i * BLK:(i + 1) * BLK] = (acc[:, i * BLK:(i + 1) * BLK] * f).astype(BF16)


    def pieces_perm():
        def column():
            ocol[...] = jnp.broadcast_to(order[...].reshape(1, TOK), (BLK, TOK)).astype(F32).T

        def block(q, p):
            lane = lax.broadcasted_iota(jnp.int32, (PLANE, BLK), 1).astype(F32)
            o = ocol[pl.ds(pl.multiple_of(zrel(RHO[q][p]) * PLANE, 32), PLANE), :]
            for j in range(TOK // BLK):
                perm[rows_of(q, p), j * BLK:(j + 1) * BLK] = jnp.where(o == lane + float(j * BLK), 1.0, 0.0).astype(BF16)

        return [column] + [functools.partial(block, q, p) for q in range(NQ) for p in range(2)]

    def pieces_transpose():
        def one(j):
            wgut[j * 256:(j + 1) * 256, :] = wgu[j].astype(F32).T.astype(BF16)

        return [functools.partial(one, j) for j in range(NY)]

    def make_perm():
        for piece in pieces_perm():
            piece()

    def pieces_masks():
        def wait():
            for cp in loads[2:]:
                cp.wait()

        return [wait] + [functools.partial(masks, i, i + 1) for i in range(DW // BLK)]

    T.start()
    G.start()
    T.step(1, pieces_masks()[:4])
    G.step(1, pieces_masks()[4:])
    T.step(2, pieces_perm()[:5])
    G.step(2, pieces_perm()[5:])
    T.step(3, pieces_transpose())
    G.step(3, pieces_p(0))
    T.step(4, pieces_g(0))
    stage_c(0)
    G.step(4, pieces_p(1))
    T.step(5, pieces_g(1))
    stage_c(1)
    G.step(5, pieces_p(2))
    gpair(2)
    gpair(3)
    dh_partial()
    stage_p(3)
    stage_c(2)
    dh_pair()
    stage_c(3)
    permute()
    transpose_tokens()
    dh_total()
    stage_y(2)
    stage_y(1)
    stage_a(2)
    stage_y(3)
    stage_a(1)
    stage_b(2)
    stage_y(0)
    stage_e()
    stage_a(3)
    stage_b(1)
    stage_a(0)
    stage_b(3)
    stage_x(2)
    stage_b(0)
    stage_x(1)
    stage_f()
    weight_grads(0, 2)
    stage_x(3)
    stage_k()
    down_grads(0, 1)
    stage_x(0)
    weight_grads(2, 4)
    down_grads(1, 4)
    for d in (1, 7, 2, 6, 3, 5, 4):
        rz_copy(d, zsrc.at[0, 0]).wait_recv()
    t = zsrc[0, 0].astype(F32)
    for j in range(NZ - 1):
        t = t + zrecv[j].astype(F32)
    gin_ref[...] = jnp.concatenate([t[:ROWS], t[ROWS:]], axis=1).astype(BF16)

    for cp in started:
        cp.wait_send()


def copy_kernel(a, b, c, d, oa, ob, oc, od, sem):
    stores = []
    for src, dst, n in ((b, ob, 4), (c, oc, 4), (d, od, 4), (a, oa, 1)):
        step = src.shape[0] // n
        for i in range(n):
            rows = pl.ds(i * step, step)
            stores.append(pltpu.make_async_copy(src.at[rows], dst.at[rows], sem.at[len(stores)]))
            stores[-1].start()
    for cp in stores:
        cp.wait()


def on_device(tokens, grad_out, w_gate, w_up, w_down, block_flags, token_order):
    vmem = pl.BlockSpec(memory_space=pltpu.VMEM)
    smem = pl.BlockSpec(memory_space=pltpu.SMEM)
    hbm = pl.BlockSpec(memory_space=pl.ANY)
    V = pltpu.VMEM
    n = NZ * NX
    half_slab = (n, 2 * ROWS, DW // 4)
    sems = [5]
    for _ in range(2):
        for m in (3, 8 * NP, 8, 24):
            sems += [m, m]
    for m in (NQ, 3 * NQ, 4, 3 * NQ, 4 * NQ, 6 * NQ, 7, 3, 4):
        sems += [m, m]
    scratch = [
        V((ROWS, DW), BF16), V((ROWS, DW), BF16),
        V((DW, FW), BF16), V((DW, FW), BF16), V((FW, DW), BF16),
        V((NY, DW, 2 * BLK), BF16), V((2 * FW, DW), BF16), V((FW, DW), BF16),
        V(half_slab, BF16), V(half_slab, BF16), V(half_slab, BF16), V(half_slab, BF16),
        V((TOK, DW), BF16), V((TOK, DW), BF16), V((TOK, DW), BF16),
        V((DW, TOK), BF16), V((TOK, TOK), BF16), V((TOK, BLK), F32),
        V((NQ, NY, 2 * PLANE, 2 * BLK), BF16), V((NQ, NY, PLANE, 2 * BLK), BF16),
        V((NQ, NY - 1, PLANE, 2 * BLK), BF16), V((NQ, NY - 1, PLANE, 2 * BLK), BF16),
        V((TOK, FW), BF16), V((NY, TOK, BLK), BF16), V((NY, HALF, BLK), BF16),
        V((NY - 1, HALF, BLK), BF16), V((NY - 1, HALF, BLK), BF16), V((HALF, BLK), F32),
        V((TOK, 2 * FW), BF16), V((NY, TOK, BLK), BF16), V((BLK, TOK), BF16),
        V((2, 2 * PLANE, DW), F32),
        V((NQ, NX, 2) + SLAB, BF16), V((NQ, NX - 1, 2) + SLAB, BF16),
        V((NQ, 2) + SLAB, BF16), V((NZ - 1,) + SLAB, BF16),
    ] + [pltpu.SemaphoreType.DMA((m,)) for m in sems]
    out_shape = (
        jax.ShapeDtypeStruct((ROWS, DW), BF16),
        jax.ShapeDtypeStruct((DW, FW), BF16),
        jax.ShapeDtypeStruct((DW, FW), BF16),
        jax.ShapeDtypeStruct((FW, DW), BF16),
    )
    out = pl.pallas_call(
        kernel,
        out_shape=tuple(pltpu.VMEM(o.shape, o.dtype) for o in out_shape),
        in_specs=[hbm, hbm, hbm, hbm, hbm, smem, vmem],
        out_specs=(vmem,) * 4,
        scratch_shapes=scratch,
        compiler_params=pltpu.CompilerParams(
            collective_id=0, has_side_effects=True, vmem_limit_bytes=57 * 2**20),
        name="layer_backward",
    )(tokens, grad_out, w_gate, w_up, w_down, block_flags.T, token_order)
    return pl.pallas_call(
        copy_kernel,
        out_shape=out_shape,
        in_specs=[vmem] * 4,
        out_specs=(hbm,) * 4,
        scratch_shapes=[pltpu.SemaphoreType.DMA((13,))],
        compiler_params=pltpu.CompilerParams(vmem_limit_bytes=16 * 2**20),
        name="hand_over",
    )(*out)


def solution(mesh):
    return jax.shard_map(
        on_device,
        mesh=mesh,
        in_specs=(
            P("col", "row"), P("col", "row"), P("row", "col"), P("row", "col"),
            P("col", "row"), P("row", "col"), P(),
        ),
        out_specs=(P("col", "row"), P("row", "col"), P("row", "col"), P("col", "row")),
        check_vma=False,
    )
```
